32 devices in a mesh: seq: 8 (over z, core), fsdp: 4 (over y, x).
Axes of the slice: x: 2, y: 2, z: 4, core: 2. Of those that a mesh axis runs over, the one named last changes fastest.
Arguments:
- hidden_in: bfloat16 [8, 2048, 1024], P('fsdp', 'seq'), may hold values from -6 to 6
- norm1_gain: bfloat16 [1024], P(('seq', 'fsdp')), may hold values from 0.5 to 1.5
- norm1_bias: bfloat16 [1024], P(('seq', 'fsdp')), may hold values from -1.75 to 1.75
- qkv_weight: bfloat16 [1024, 3072], P(('seq', 'fsdp')), may hold values from -0.1875 to 0.1875
- qv_bias: bfloat16 [2048], P(('seq', 'fsdp')), may hold values from -1.75 to 1.75
- alibi_slopes: float32 [16], replicated, may hold values from 0.00048828125 to 0.2
- out_weight: bfloat16 [1024, 1024], P(('seq', 'fsdp')), may hold values from -0.75 to 0.75
- out_bias: bfloat16 [1024], P(('seq', 'fsdp')), may hold values from -1.75 to 1.75
- norm2_gain: bfloat16 [1024], P(('seq', 'fsdp')), may hold values from 0.5 to 1.5
- norm2_bias: bfloat16 [1024], P(('seq', 'fsdp')), may hold values from -1.75 to 1.75
- up_weight: bfloat16 [1024, 4096], P(('seq', 'fsdp')), may hold values from -0.1875 to 0.1875
- up_bias: bfloat16 [4096], P(('seq', 'fsdp')), may hold values from -1.75 to 1.75
- down_weight: bfloat16 [4096, 1024], P(('seq', 'fsdp')), may hold values from -0.09375 to 0.09375
- down_bias: bfloat16 [1024], P(('seq', 'fsdp')), may hold values from -1.75 to 1.75
- out_grad: bfloat16 [8, 2048, 1024], P('fsdp', 'seq'), may hold values from -6 to 6
Outputs:
- block_out: bfloat16 [8, 2048, 1024], P('fsdp', 'seq')
- input_grad: float32 [8, 2048, 1024], P('fsdp', 'seq')
- grad_norm1_gain: float32 [1024], P(('seq', 'fsdp'))
- grad_norm1_bias: float32 [1024], P(('seq', 'fsdp'))
- grad_qkv_weight: float32 [1024, 3072], P(('seq', 'fsdp'))
- grad_qv_bias: float32 [2048], P(('seq', 'fsdp'))
- grad_out_weight: float32 [1024, 1024], P(('seq', 'fsdp'))
- grad_out_bias: float32 [1024], P(('seq', 'fsdp'))
- grad_norm2_gain: float32 [1024], P(('seq', 'fsdp'))
- grad_norm2_bias: float32 [1024], P(('seq', 'fsdp'))
- grad_up_weight: float32 [1024, 4096], P(('seq', 'fsdp'))
- grad_up_bias: float32 [4096], P(('seq', 'fsdp'))
- grad_down_weight: float32 [4096, 1024], P(('seq', 'fsdp'))
- grad_down_bias: float32 [1024], P(('seq', 'fsdp'))
The draws below stay inside these ranges and needn't reach their ends.
All inputs are finite; a program needn't handle non-finite values.
Results may differ from the reference program's by a relative error of at most 0.0095.
Values may be sent and summed in bfloat16 or wider, within the bound.
No kernel may reach another device: no remote copies, remote signals or barrier semaphores. Data moves between devices by JAX's collectives and lax.ppermute only.
A program may use at most 192 MiB of HBM per device.

```python
import math
import jax
import jax.numpy as jnp
from jax import lax

D = 1024
H = 16
HD = 64
FF = 4096
SEQ_LEN = 2048
BATCH = 8


def levels(own_key, dims, split, smallest, top_value):
    gain, own = 1.0, jax.random.fold_in(own_key, 6)
    for position, shards_of in split:
        steps = jnp.exp(jax.random.uniform(jax.random.fold_in(own, position), (shards_of,), jnp.float32, smallest / len(split), top_value / len(split)))
        gain = gain * jnp.repeat(steps, dims[position] // shards_of).reshape([-1 if axis == position else 1 for axis in range(len(dims))])
    return gain


def centred(rng, shape, deviation, reach, cuts=(), held_as=jnp.bfloat16):
    gain = levels(rng, shape, cuts, -0.22, 0.18) if cuts else 1.0
    drawn = jax.random.normal(rng, shape, jnp.float32) * deviation * gain
    return jnp.minimum(jnp.maximum(drawn, -reach), reach).astype(held_as)


def setup_inputs(seed: int = 0) -> dict:
    key_of = jax.random.split(jax.random.key(seed), 16)
    return {
        "hidden_in": centred(key_of[0], (BATCH, SEQ_LEN, D), 1.0, 6.0, ((0, 4), (1, 8))),
        "norm1_gain": jnp.clip(1.0 + 0.1 * jax.random.normal(key_of[1], (D,), jnp.float32), 0.5, 1.5).astype(jnp.bfloat16),
        "norm1_bias": centred(key_of[2], (D,), 0.3, 1.75, ((0, 32),)),
        "qkv_weight": centred(key_of[3], (D, 3 * D), D ** -0.5, 0.1875, ((0, 32),)),
        "qv_bias": centred(key_of[4], (2 * D,), 0.3, 1.75, ((0, 32),)),
        "alibi_slopes": jnp.clip(jnp.exp(jax.random.uniform(key_of[5], (H,), jnp.float32, math.log(0.00048828125), math.log(0.2))), 0.00048828125, 0.2),
        "out_weight": centred(key_of[6], (D, D), (D // 16) ** -0.5, 0.75, ((0, 32),)),
        "out_bias": centred(key_of[7], (D,), 0.3, 1.75, ((0, 32),)),
        "norm2_gain": jnp.clip(1.0 + 0.1 * jax.random.normal(key_of[8], (D,), jnp.float32), 0.5, 1.5).astype(jnp.bfloat16),
        "norm2_bias": centred(key_of[9], (D,), 0.3, 1.75, ((0, 32),)),
        "up_weight": centred(key_of[10], (D, FF), D ** -0.5, 0.1875, ((0, 32),)),
        "up_bias": centred(key_of[11], (FF,), 0.3, 1.75, ((0, 32),)),
        "down_weight": centred(key_of[12], (FF, D), FF ** -0.5, 0.09375, ((0, 32),)),
        "down_bias": centred(key_of[13], (D,), 0.3, 1.75, ((0, 32),)),
        "out_grad": centred(key_of[14], (BATCH, SEQ_LEN, D), 1.0, 6.0, ((0, 4), (1, 8))),
    }


@jax.custom_vjp
def low(v):
    return lax.optimization_barrier(v.astype(jnp.bfloat16)).astype(jnp.float32)

@jax.custom_vjp
def low_back(v):
    return v

def low_keep(v):
    return (low(v), None)

def low_pass(kept, grad):
    return (grad,)

def back_keep(v):
    return (v, None)

def back_low(kept, grad):
    return (low(grad),)
low.defvjp(low_keep, low_pass)
low_back.defvjp(back_keep, back_low)

def layer_norm(values, norm_gain, norm_shift):
    average = lax.optimization_barrier(jnp.mean(values, -1, keepdims=True))
    centered = values - average
    variance = lax.optimization_barrier(jnp.mean(centered * centered, -1, keepdims=True))
    return centered * lax.rsqrt(variance + 1e-05) * norm_gain + norm_shift

def gelu_tanh(values):
    inside = 0.7978845608 * (values + 0.044715 * values * values * values)
    return 0.5 * values * (1.0 + jnp.tanh(inside))

def forward(inputs, slopes, first_gain, first_shift, w_qkv, bias_qv, w_out, b_out, second_gain, second_shift, w_up, b_up, w_down, b_down):
    highest = lax.Precision.HIGHEST
    group_size, length, model_width = inputs.shape
    first_norm = low(layer_norm(inputs, first_gain, first_shift))
    full_bias = jnp.concatenate([bias_qv[:model_width], jnp.zeros((model_width,), jnp.float32), bias_qv[model_width:]])
    projected = jnp.einsum('gld,de->gle', first_norm, w_qkv, precision=highest) + full_bias
    projected = low_back(low(projected))
    heads = projected.reshape(group_size, length, 3, H, HD).transpose(2, 0, 3, 1, 4)
    queries = heads[0]
    keys_all = heads[1]
    values_all = heads[2]
    row_block = min(512, length)
    num_blocks = length // row_block
    key_pos = jnp.arange(length, dtype=jnp.int32)
    factor = HD ** (-0.5)

    @jax.checkpoint
    def one_block(number):
        offset = number * row_block
        query_rows = lax.dynamic_slice_in_dim(queries, offset, row_block, 2)
        raw_scores = jnp.einsum('ghqd,ghkd->ghqk', query_rows, keys_all, precision=highest) * factor
        query_pos = offset + jnp.arange(row_block, dtype=jnp.int32)
        distance = query_pos[:, None] - key_pos[None, :]
        raw_scores = raw_scores - slopes[None, :, None, None] * distance.astype(jnp.float32)
        scores = jnp.where(distance >= 0, low_back(raw_scores), -1e+30)
        attn_probs = low(jax.nn.softmax(scores, -1))
        return jnp.einsum('ghqk,ghkd->ghqd', attn_probs, values_all, precision=highest)
    blended = lax.map(one_block, jnp.arange(num_blocks, dtype=jnp.int32))
    attended = blended.transpose(1, 0, 3, 2, 4).reshape(group_size, length, model_width)
    attended = low_back(low(attended))
    branch = jnp.einsum('gld,de->gle', attended, w_out, precision=highest) + b_out
    middle = inputs + low_back(branch)
    second_norm = low(layer_norm(middle, second_gain, second_shift))
    hidden_pre = low_back(jnp.einsum('gld,df->glf', second_norm, w_up, precision=highest) + b_up)
    activated = low(gelu_tanh(hidden_pre))
    return middle + jnp.einsum('glf,fd->gld', activated, w_down, precision=highest) + b_down

def reference(hidden_in, norm1_gain, norm1_bias, qkv_weight, qv_bias, alibi_slopes, out_weight, out_bias, norm2_gain, norm2_bias, up_weight, up_bias, down_weight, down_bias, out_grad):
    params = tuple((item.astype(jnp.float32) for item in (norm1_gain, norm1_bias, qkv_weight, qv_bias, out_weight, out_bias, norm2_gain, norm2_bias, up_weight, up_bias, down_weight, down_bias)))
    slopes = alibi_slopes.astype(jnp.float32)
    num_seqs = hidden_in.shape[0]
    group_size = math.gcd(num_seqs, max(1, 4096 // SEQ_LEN))
    num_groups = num_seqs // group_size
    inputs = hidden_in.astype(jnp.float32).reshape(num_groups, group_size, SEQ_LEN, D)
    cotangent = out_grad.astype(jnp.float32).reshape(num_groups, group_size, SEQ_LEN, D)

    def apply_layer(values, *weights):
        return forward(values, slopes, *weights)

    def group_step(running, members):
        group_inputs, group_cot = members
        outputs, pullback = jax.vjp(apply_layer, group_inputs, *params)
        gradients = pullback(group_cot)
        running = tuple((total + grad for total, grad in zip(running, gradients[1:])))
        return (running, (outputs.astype(jnp.bfloat16), gradients[0]))
    initial = tuple((jnp.zeros_like(item) for item in params))
    totals, (outputs, input_grads) = lax.scan(group_step, initial, (inputs, cotangent))
    block_out = outputs.reshape(num_seqs, SEQ_LEN, D)
    input_grad = input_grads.reshape(num_seqs, SEQ_LEN, D)
    return (block_out, input_grad, totals[0], totals[1], totals[2], totals[3], totals[4], totals[5], totals[6], totals[7], totals[8], totals[9], totals[10], totals[11])
```

```python
import functools

import jax
import jax.numpy as jnp
from jax import lax
from jax.experimental import pallas as pl
from jax.experimental.pallas import tpu as pltpu
from jax.sharding import Mesh
from jax.sharding import PartitionSpec as P

H = 16
HD = 64
SEQ = ("z", "core")
FSDP = ("fy", "fx")
ALL = SEQ + FSDP
BF = jnp.bfloat16
F32 = jnp.float32
NT = (((1,), (1,)), ((), ()))
VMEM_BYTES = 48 * 1024 * 1024


def layer_norm(values, norm_gain, norm_shift):
    average = jnp.mean(values, -1, keepdims=True)
    centered = values - average
    variance = jnp.mean(centered * centered, -1, keepdims=True)
    return centered * lax.rsqrt(variance + 1e-05) * norm_gain + norm_shift


def gelu_tanh(values):
    inside = 0.7978845608 * (values + 0.044715 * values * values * values)
    return 0.5 * values * (1.0 + jnp.tanh(inside))


def outer_sum(left, right):
    return lax.dot_general(left, right, (((0,), (0,)), ((), ())), preferred_element_type=F32)


def times_rows(left, right):
    return lax.dot_general(left, right, NT, preferred_element_type=F32)


def swap(values, axis):
    return lax.ppermute(values, axis, [(0, 1), (1, 0)])


def gather_axis(values, axis):
    if lax.axis_size(axis) != 2:
        return lax.all_gather(values, axis, axis=0, tiled=False)
    other = swap(values, axis)
    first = lax.axis_index(axis) == 0
    return jnp.stack([jnp.where(first, values, other), jnp.where(first, other, values)])


def reduce_axis(values, axis, position):
    if lax.axis_size(axis) != 2:
        return lax.psum_scatter(values, axis, scatter_dimension=position, tiled=False)
    me = lax.axis_index(axis)
    give = lax.dynamic_index_in_dim(values, 1 - me, position, keepdims=False)
    keep = lax.dynamic_index_in_dim(values, me, position, keepdims=False)
    return (keep.astype(F32) + swap(give, axis).astype(F32)).astype(BF)


def project_kernel(x_ref, gain_ref, shift_ref, w_ref, bias_ref, low_ref, q_ref, k_ref, v_ref, kt_ref, vt_ref):
    width = q_ref.shape[1]
    low = layer_norm(x_ref[...].astype(F32), gain_ref[...], shift_ref[...]).astype(BF)
    low_ref[...] = low
    made = (jnp.dot(low, w_ref[...], preferred_element_type=F32) + bias_ref[...]).astype(BF)
    made = made.astype(F32)
    keys, values = made[:, width : 2 * width], made[:, 2 * width :]
    q_ref[...] = (made[:, :width] * (HD**-0.5)).astype(BF)
    k_ref[...] = keys.astype(BF)
    v_ref[...] = values.astype(BF)
    kt_ref[...] = keys.T.astype(BF)
    vt_ref[...] = values.T.astype(BF)


def project(rows, gain, shift, weight, bias):
    length, model_width = rows.shape
    width = weight.shape[1] // 3
    block = min(512, length)
    whole = lambda i: (0, 0)
    down = lambda i: (i, 0)
    across = lambda i: (0, i)
    return pl.pallas_call(
        project_kernel,
        grid=(length // block,),
        in_specs=[
            pl.BlockSpec((block, model_width), down),
            pl.BlockSpec((1, model_width), whole),
            pl.BlockSpec((1, model_width), whole),
            pl.BlockSpec((model_width, 3 * width), whole),
            pl.BlockSpec((1, 3 * width), whole),
        ],
        out_specs=[
            pl.BlockSpec((block, model_width), down),
            pl.BlockSpec((block, width), down),
            pl.BlockSpec((block, width), down),
            pl.BlockSpec((block, width), down),
            pl.BlockSpec((width, block), across),
            pl.BlockSpec((width, block), across),
        ],
        out_shape=[jax.ShapeDtypeStruct((length, model_width), BF)]
        + [jax.ShapeDtypeStruct((length, width), BF)] * 3
        + [jax.ShapeDtypeStruct((width, length), BF)] * 2,
        compiler_params=pltpu.CompilerParams(vmem_limit_bytes=VMEM_BYTES),
        cost_estimate=pl.CostEstimate(
            flops=2 * length * model_width * 3 * width,
            bytes_accessed=4 * length * model_width + 10 * length * width,
            transcendentals=0,
        ),
        name="project",
    )(rows, gain, shift, weight, bias)


def tile_helpers(head, slope, block, width):
    lane = lax.broadcasted_iota(jnp.int32, (block, width), 1)
    mine = (lane >= head * HD) & (lane < head * HD + HD)
    key = lax.broadcasted_iota(jnp.int32, (block, block), 0)
    query = lax.broadcasted_iota(jnp.int32, (block, block), 1)
    return mine, slope * key.astype(F32), key <= query


def attend_kernel(slope_ref, q_ref, k_ref, vt_ref, o_ref, lse_ref, score_scr, out_scr):
    block, width = q_ref.shape
    number, head = pl.program_id(0), pl.program_id(1)
    slope = slope_ref[head]
    mine, bias, causal = tile_helpers(head, slope, block, width)
    queries = jnp.where(mine, q_ref[...], jnp.zeros_like(q_ref[...]))

    def one_block(last):
        highest = None
        for t in range(last + 1):
            rows = pl.ds(t * block, block)
            scores = lax.dot_general(k_ref[rows, :], queries, NT, preferred_element_type=F32) + bias
            if t == last:
                scores = jnp.where(causal, scores, -1e30)
            score_scr[rows, :] = scores
            top = jnp.max(scores, 0, keepdims=True) + slope * (t * block)
            highest = top if highest is None else jnp.maximum(highest, top)
        total = jnp.zeros((1, block), F32)
        blended = jnp.zeros((width, block), F32)
        for t in range(last + 1):
            rows = pl.ds(t * block, block)
            weights = jnp.exp(score_scr[rows, :] - (highest - slope * (t * block)))
            total = total + jnp.sum(weights, 0, keepdims=True)
            blended = blended + jnp.dot(
                vt_ref[:, rows], weights.astype(BF), preferred_element_type=F32
            )
        lse_ref[...] = (highest + jnp.log(total)).reshape(lse_ref.shape)
        result = jnp.where(mine, (blended / total).T, 0.0)

        @pl.when(head == 0)
        def _():
            out_scr[...] = result

        @pl.when(head > 0)
        def _():
            out_scr[...] = out_scr[...] + result

    for last in range(k_ref.shape[0] // block):
        pl.when(number == last)(functools.partial(one_block, last))

    @pl.when(head == pl.num_programs(1) - 1)
    def _():
        o_ref[...] = out_scr[...].astype(BF)


def attend(slopes, queries, keys, values_t):
    length, width = queries.shape
    heads = slopes.shape[0]
    block = min(256, length)
    whole = lambda i, h: (0, 0)
    down = lambda i, h: (i, 0)
    return pl.pallas_call(
        attend_kernel,
        grid=(length // block, heads),
        in_specs=[
            pl.BlockSpec(memory_space=pltpu.SMEM),
            pl.BlockSpec((block, width), down),
            pl.BlockSpec((length, width), whole),
            pl.BlockSpec((width, length), whole),
        ],
        out_specs=[
            pl.BlockSpec((block, width), down),
            pl.BlockSpec((1, 1, block), lambda i, h: (h, 0, i)),
        ],
        out_shape=[
            jax.ShapeDtypeStruct((length, width), BF),
            jax.ShapeDtypeStruct((heads, 1, length), F32),
        ],
        scratch_shapes=[pltpu.VMEM((length, block), F32), pltpu.VMEM((block, width), F32)],
        compiler_params=pltpu.CompilerParams(vmem_limit_bytes=VMEM_BYTES),
        cost_estimate=pl.CostEstimate(
            flops=8 * heads * length * length * HD,
            bytes_accessed=8 * length * width,
            transcendentals=heads * length * length // 2,
        ),
        name="attend",
    )(slopes, queries, keys, values_t)


def attend_back_kernel(
    slope_ref, q_ref, k_ref, kt_ref, v_ref, g_ref, lse_ref,
    dq_ref, dk_ref, dv_ref, prob_scr, dp_scr, dk_scr, dv_scr, dq_scr,
):
    block, width = q_ref.shape
    number, head = pl.program_id(0), pl.program_id(1)
    slope = slope_ref[head]
    mine, bias, causal = tile_helpers(head, slope, block, width)
    queries = jnp.where(mine, q_ref[...], jnp.zeros_like(q_ref[...]))
    grads = jnp.where(mine, g_ref[...], jnp.zeros_like(g_ref[...]))
    lse = lse_ref[...].reshape(1, block)

    @pl.when((number == 0) & (head == 0))
    def _():
        dk_scr[...] = jnp.zeros_like(dk_scr)
        dv_scr[...] = jnp.zeros_like(dv_scr)

    def one_block(last):
        centre = jnp.zeros((1, block), F32)
        for t in range(last + 1):
            rows = pl.ds(t * block, block)
            scores = lax.dot_general(k_ref[rows, :], queries, NT, preferred_element_type=F32) + bias
            if t == last:
                scores = jnp.where(causal, scores, -1e30)
            probs = jnp.exp(scores - (lse - slope * (t * block)))
            dp = lax.dot_general(v_ref[rows, :], grads, NT, preferred_element_type=F32)
            prob_scr[rows, :] = probs
            dp_scr[rows, :] = dp
            centre = centre + jnp.sum(probs * dp, 0, keepdims=True)
            dv_scr[rows, :] = dv_scr[rows, :] + jnp.dot(
                probs.astype(BF), grads, preferred_element_type=F32
            )
        dq = jnp.zeros((width, block), F32)
        for t in range(last + 1):
            rows = pl.ds(t * block, block)
            ds = (prob_scr[rows, :] * (dp_scr[rows, :] - centre)).astype(BF)
            dk_scr[rows, :] = dk_scr[rows, :] + jnp.dot(ds, queries, preferred_element_type=F32)
            dq = dq + jnp.dot(kt_ref[:, rows], ds, preferred_element_type=F32)
        result = jnp.where(mine, (dq * (HD**-0.5)).T, 0.0)

        @pl.when(head == 0)
        def _():
            dq_scr[...] = result

        @pl.when(head > 0)
        def _():
            dq_scr[...] = dq_scr[...] + result

    for last in range(k_ref.shape[0] // block):
        pl.when(number == last)(functools.partial(one_block, last))

    @pl.when(head == pl.num_programs(1) - 1)
    def _():
        dq_ref[...] = dq_scr[...].astype(BF)

    @pl.when((head == pl.num_programs(1) - 1) & (number == pl.num_programs(0) - 1))
    def _():
        dk_ref[...] = dk_scr[...].astype(BF)
        dv_ref[...] = dv_scr[...].astype(BF)


def attend_back(slopes, queries, keys, keys_t, values, grads, lse):
    length, width = queries.shape
    heads = slopes.shape[0]
    block = min(256, length)
    whole = lambda i, h: (0, 0)
    down = lambda i, h: (i, 0)
    return pl.pallas_call(
        attend_back_kernel,
        grid=(length // block, heads),
        in_specs=[
            pl.BlockSpec(memory_space=pltpu.SMEM),
            pl.BlockSpec((block, width), down),
            pl.BlockSpec((length, width), whole),
            pl.BlockSpec((width, length), whole),
            pl.BlockSpec((length, width), whole),
            pl.BlockSpec((block, width), down),
            pl.BlockSpec((1, 1, block), lambda i, h: (h, 0, i)),
        ],
        out_specs=[
            pl.BlockSpec((block, width), down),
            pl.BlockSpec((length, width), whole),
            pl.BlockSpec((length, width), whole),
        ],
        out_shape=[jax.ShapeDtypeStruct((length, width), BF)] * 3,
        scratch_shapes=[
            pltpu.VMEM((length, block), F32),
            pltpu.VMEM((length, block), F32),
            pltpu.VMEM((length, width), F32),
            pltpu.VMEM((length, width), F32),
            pltpu.VMEM((block, width), F32),
        ],
        compiler_params=pltpu.CompilerParams(vmem_limit_bytes=VMEM_BYTES),
        cost_estimate=pl.CostEstimate(
            flops=20 * heads * length * length * HD,
            bytes_accessed=16 * length * width,
            transcendentals=heads * length * length // 2,
        ),
        name="attend_back",
    )(slopes, queries, keys, keys_t, values, grads, lse)


def body(
    hidden_in,
    norm1_gain,
    norm1_bias,
    qkv_weight,
    qv_bias,
    alibi_slopes,
    out_weight,
    out_bias,
    norm2_gain,
    norm2_bias,
    up_weight,
    up_bias,
    down_weight,
    down_bias,
    out_grad,
):
    seq_devices = lax.axis_size(SEQ)
    fsdp_devices = lax.axis_size(FSDP)
    devices = seq_devices * fsdp_devices
    z_size, y_size, x_size = lax.axis_size("z"), lax.axis_size("fy"), lax.axis_size("fx")
    sequences, local_len, model_width = hidden_in.shape
    tokens = sequences * local_len
    heads_local = H // seq_devices
    width = heads_local * HD
    ff_width = up_weight.shape[1]
    rows_each = qkv_weight.shape[0]
    ff_each = down_weight.shape[0]
    up_blocks = ff_width // model_width
    place = lax.axis_index(SEQ)
    slopes = lax.dynamic_slice_in_dim(alibi_slopes, place * heads_local, heads_local)

    up_stack = up_weight.reshape(rows_each, up_blocks, model_width).transpose(1, 0, 2)
    stacked = jnp.concatenate(
        [out_weight, down_weight, up_stack.reshape(up_blocks * rows_each, model_width)], 0
    )
    along_z = lax.all_gather(stacked, "z", axis=0, tiled=False)
    cut = rows_each + ff_each
    low_part, up_part = along_z[:, :cut], along_z[:, cut:]
    up_part = gather_axis(gather_axis(gather_axis(up_part, "fx"), "fy"), "core")
    low_part = gather_axis(gather_axis(gather_axis(low_part, "fy"), "fx"), "core")
    up_part = up_part.reshape(2, y_size, x_size, z_size, up_blocks, rows_each, model_width)
    w_up = up_part.transpose(3, 0, 1, 2, 5, 4, 6).reshape(model_width, ff_width)
    low_part = low_part.transpose(3, 0, 2, 1, 4, 5)
    w_out = low_part[:, :, :, :, :rows_each].reshape(model_width, model_width)
    w_down = low_part[:, :, :, :, rows_each:].reshape(ff_width, model_width)

    small_parts = (norm1_gain, norm1_bias, qv_bias, out_bias, norm2_gain, norm2_bias, up_bias, down_bias)
    small_all = lax.all_gather(jnp.concatenate(small_parts), ALL, axis=0, tiled=False)
    full, start = [], 0
    for part in small_parts:
        size = part.shape[0]
        full.append(small_all[:, start : start + size].reshape(-1).astype(F32))
        start += size
    first_gain, first_shift, bias_qv, b_out, second_gain, second_shift, b_up, b_down = full

    columns = qkv_weight.reshape(rows_each, 3, seq_devices, width).transpose(2, 0, 1, 3)
    columns = columns.reshape(seq_devices, rows_each, 3 * width)
    columns = lax.all_to_all(columns, SEQ, split_axis=0, concat_axis=0, tiled=True)
    w_heads = lax.all_gather(columns, FSDP, axis=1, tiled=False).reshape(model_width, 3 * width)
    bias_parts = bias_qv.reshape(2, seq_devices, width)
    bias_mine = lax.dynamic_index_in_dim(bias_parts, place, 1, keepdims=False)
    bias_heads = jnp.concatenate([bias_mine[0], jnp.zeros((width,), F32), bias_mine[1]])

    kept = []
    returned = []
    for n in range(sequences):
        rows = lax.all_gather(hidden_in[n], SEQ, axis=0, tiled=True)
        first_low, q, k, v, kt, vt = project(
            rows, first_gain[None], first_shift[None], w_heads, bias_heads[None]
        )
        attended, lse = attend(slopes, q, k, vt)
        returned.append(lax.all_to_all(attended, SEQ, split_axis=0, concat_axis=1, tiled=True))
        kept.append((first_low, q, k, v, kt, lse))
    attended_low = jnp.stack(returned).reshape(tokens, model_width)

    flat_in = hidden_in.reshape(tokens, model_width).astype(F32)
    middle = flat_in + jnp.dot(attended_low, w_out, preferred_element_type=F32) + b_out
    second_norm, second_back = jax.vjp(layer_norm, middle, second_gain, second_shift)
    second_low = second_norm.astype(BF)
    hidden_pre = jnp.dot(second_low, w_up, preferred_element_type=F32) + b_up
    activated, gelu_back = jax.vjp(gelu_tanh, hidden_pre)
    activated_low = activated.astype(BF)
    result = middle + jnp.dot(activated_low, w_down, preferred_element_type=F32) + b_down
    block_out = result.astype(BF).reshape(sequences, local_len, model_width)

    cot_low = out_grad.reshape(tokens, model_width)
    cotangent = cot_low.astype(F32)
    grad_act = times_rows(cot_low, w_down)
    (grad_pre,) = gelu_back(grad_act)
    grad_hidden = grad_pre.astype(BF)
    grad_second = times_rows(grad_hidden, w_up)
    grad_mid_norm, grad_gain_two, grad_shift_two = second_back(grad_second)
    grad_middle = cotangent + grad_mid_norm
    grad_branch = grad_middle.astype(BF)
    grad_attended = times_rows(grad_branch, w_out).astype(BF)
    grad_attended = grad_attended.reshape(sequences, local_len, model_width)
    grad_heads = [
        lax.all_to_all(grad_attended[n], SEQ, split_axis=1, concat_axis=0, tiled=True)
        for n in range(sequences)
    ]

    grad_down = outer_sum(activated_low, cot_low).astype(BF)
    grad_up = outer_sum(second_low, grad_hidden).astype(BF)
    grad_outw = outer_sum(attended_low, grad_branch).astype(BF)

    split = (z_size, 2, y_size, x_size)
    sum_down = grad_down.reshape(*split, ff_each, model_width)
    sum_down = reduce_axis(reduce_axis(reduce_axis(sum_down, "core", 1), "fx", 2), "fy", 1)
    sum_up = grad_up.reshape(*split, rows_each, ff_width)
    sum_up = reduce_axis(reduce_axis(reduce_axis(sum_up, "core", 1), "fy", 1), "fx", 1)
    sum_out = grad_outw.reshape(*split, rows_each, model_width)
    sum_out = reduce_axis(reduce_axis(reduce_axis(sum_out, "core", 1), "fx", 2), "fy", 1)
    sum_up = sum_up.reshape(z_size, rows_each, up_blocks, model_width).transpose(0, 2, 1, 3)
    sum_up = sum_up.reshape(z_size, up_blocks * rows_each, model_width)
    sums = lax.psum_scatter(
        jnp.concatenate([sum_out, sum_down, sum_up], 1), "z", scatter_dimension=0, tiled=False
    ).astype(F32)
    out_outw = sums[:rows_each]
    out_down = sums[rows_each:cut]
    out_up = sums[cut:].reshape(up_blocks, rows_each, model_width).transpose(1, 0, 2)
    out_up = out_up.reshape(rows_each, ff_width)

    rear = [
        jnp.sum(grad_branch.astype(F32), 0),
        grad_gain_two,
        grad_shift_two,
        jnp.sum(grad_hidden.astype(F32), 0),
        jnp.sum(cotangent, 0),
    ]
    rear_wide = jnp.concatenate([part.reshape(devices, -1) for part in rear], 1)
    rear_sum = jnp.sum(lax.all_to_all(rear_wide, ALL, split_axis=0, concat_axis=0, tiled=True), 0)

    grad_qkvw = jnp.zeros((model_width, 3 * width), F32)
    column_sums = jnp.zeros((3 * width,), F32)
    grad_first = []
    for n in range(sequences):
        first_low, q, k, v, kt, lse = kept[n]
        dq, dk, dv = attend_back(slopes, q, k, kt, v, grad_heads[n], lse)
        grad_projected = jnp.concatenate([dq, dk, dv], 1)
        partial = times_rows(grad_projected, w_heads).astype(BF)
        grad_first.append(lax.psum_scatter(partial, SEQ, scatter_dimension=0, tiled=True))
        grad_qkvw = grad_qkvw + outer_sum(first_low, grad_projected)
        column_sums = column_sums + jnp.sum(grad_projected.astype(F32), 0)
    grad_first = jnp.stack(grad_first).reshape(tokens, model_width).astype(F32)
    _, first_back = jax.vjp(layer_norm, flat_in, first_gain, first_shift)
    grad_in_norm, grad_gain_one, grad_shift_one = first_back(grad_first)
    input_grad = (grad_middle + grad_in_norm).reshape(sequences, local_len, model_width)

    wide = grad_qkvw.reshape(seq_devices, fsdp_devices, rows_each, 3 * width)
    wide = lax.psum_scatter(wide, FSDP, scatter_dimension=1, tiled=False)
    wide = lax.all_to_all(wide, SEQ, split_axis=0, concat_axis=0, tiled=True)
    wide = wide.reshape(seq_devices, rows_each, 3, width).transpose(1, 2, 0, 3)
    out_qkvw = wide.reshape(rows_each, 3 * model_width)

    qv_here = jnp.zeros((2, seq_devices, width), F32)
    qv_mine = jnp.stack([column_sums[:width], column_sums[2 * width :]])
    qv_here = lax.dynamic_update_slice_in_dim(qv_here, qv_mine[:, None], place, 1)
    front = [grad_gain_one, grad_shift_one, qv_here.reshape(-1)]
    front_wide = jnp.concatenate([part.reshape(devices, -1) for part in front], 1)
    front_sum = jnp.sum(lax.all_to_all(front_wide, ALL, split_axis=0, concat_axis=0, tiled=True), 0)

    r = rows_each
    return (
        block_out,
        input_grad,
        front_sum[:r],
        front_sum[r : 2 * r],
        out_qkvw,
        front_sum[2 * r :],
        out_outw,
        rear_sum[:r],
        rear_sum[r : 2 * r],
        rear_sum[2 * r : 3 * r],
        out_up,
        rear_sum[3 * r : 3 * r + ff_each],
        out_down,
        rear_sum[3 * r + ff_each :],
    )


def solution(mesh):
    seq_size, fsdp_size = mesh.shape["seq"], mesh.shape["fsdp"]
    fine = Mesh(mesh.devices.reshape(seq_size // 2, 2, fsdp_size // 2, 2), ALL)
    tokens = P(FSDP, SEQ, None)
    vector = P(ALL)
    matrix = P(ALL, None)
    return jax.shard_map(
        body,
        mesh=fine,
        in_specs=(
            tokens, vector, vector, matrix, vector, P(), matrix, vector, vector, vector,
            matrix, vector, matrix, vector, tokens,
        ),
        out_specs=(
            tokens, tokens, vector, vector, matrix, vector, matrix, vector, vector, vector,
            matrix, vector, matrix, vector,
        ),
        check_vma=False,
    )
```

```python
import functools

import jax
import jax.numpy as jnp
from jax import lax
from jax.experimental import pallas as pl
from jax.experimental.pallas import tpu as pltpu
from jax.sharding import Mesh
from jax.sharding import PartitionSpec as P

H = 16
HD = 64
SEQ = ("z", "core")
FSDP = ("fy", "fx")
ALL = SEQ + FSDP
BF = jnp.bfloat16
F32 = jnp.float32
NT = (((1,), (1,)), ((), ()))
VMEM_BYTES = 48 * 1024 * 1024


def layer_norm(values, norm_gain, norm_shift):
    average = jnp.mean(values, -1, keepdims=True)
    centered = values - average
    variance = jnp.mean(centered * centered, -1, keepdims=True)
    return centered * lax.rsqrt(variance + 1e-05) * norm_gain + norm_shift


def gelu_tanh(values):
    inside = 0.7978845608 * (values + 0.044715 * values * values * values)
    return 0.5 * values * (1.0 + jnp.tanh(inside))


def outer_sum(left, right):
    return lax.dot_general(left, right, (((0,), (0,)), ((), ())), preferred_element_type=F32)


def times_rows(left, right):
    return lax.dot_general(left, right, NT, preferred_element_type=F32)


def swap(values, axis):
    return lax.ppermute(values, axis, [(0, 1), (1, 0)])


def after(values, *earlier):
    return lax.optimization_barrier((values, *earlier))[0]


def merge_pair(mine, other, axis, position):
    shape = [1] * (mine.ndim + 1)
    shape[position] = 2
    slot = jnp.arange(2).reshape(shape)
    return jnp.where(
        slot == lax.axis_index(axis), jnp.expand_dims(mine, position), jnp.expand_dims(other, position)
    )


def send_axis(values, axis, position):
    if lax.axis_size(axis) != 2:
        return lax.all_gather(values, axis, axis=position, tiled=False)
    return swap(values, axis)


def join_axis(values, other, axis, position):
    if lax.axis_size(axis) != 2:
        return other
    return merge_pair(values, other, axis, position)


def at_index(values, index, position):
    return lax.dynamic_index_in_dim(values, index, position, keepdims=False)


def total_of(terms):
    total = terms[0].astype(F32)
    for term in terms[1:]:
        total = total + term.astype(F32)
    return total


def reduce_axis(terms, axis, position):
    if lax.axis_size(axis) != 2:
        whole = total_of(terms).astype(BF)
        return [lax.psum_scatter(whole, axis, scatter_dimension=position, tiled=False)]
    me = lax.axis_index(axis)
    give = total_of([at_index(term, 1 - me, position) for term in terms]).astype(BF)
    return [at_index(term, me, position) for term in terms] + [swap(give, axis)]


def feed_kernel(
    me_ref, own_ref, oth_ref, cot_ref, up_own_ref, up_oth_ref, down_own_ref, down_oth_ref, bias_ref,
    y_ref, gs_own_ref, gs_oth_ref, gd_own_ref, gd_oth_ref, gu_own_ref, gu_oth_ref, gb_ref,
    own_t, oth_t,
):
    step = pl.program_id(0)
    half = pl.num_programs(0) // 2

    @pl.when(step == 0)
    def _():
        own_t[...] = own_ref[...].astype(F32).T.astype(BF)
        oth_t[...] = oth_ref[...].astype(F32).T.astype(BF)
        y_ref[...] = jnp.zeros_like(y_ref)
        gs_own_ref[...] = jnp.zeros_like(gs_own_ref)
        gs_oth_ref[...] = jnp.zeros_like(gs_oth_ref)

    def one(down_ref, gd_ref):
        down = down_ref[0]
        pre = jnp.dot(own_ref[...], up_own_ref[...], preferred_element_type=F32)
        pre = pre + jnp.dot(oth_ref[...], up_oth_ref[...], preferred_element_type=F32)
        pre = pre + bias_ref[...]
        square = pre * pre
        tanh = jnp.tanh(0.7978845608 * (pre + 0.044715 * pre * square))
        near = 0.5 * (1.0 + tanh)
        active = (pre * near).astype(BF)
        slope = near + 0.5 * pre * (1.0 - tanh * tanh) * (
            0.7978845608 * (1.0 + 3.0 * 0.044715 * square)
        )
        grad = lax.dot_general(cot_ref[...], down, NT, preferred_element_type=F32) * slope
        grad = grad.astype(BF)
        y_ref[...] = y_ref[...] + jnp.dot(active, down, preferred_element_type=F32)
        gd_ref[0] = outer_sum(active, cot_ref[...]).astype(BF)
        gu_own_ref[...] = jnp.dot(own_t[...], grad, preferred_element_type=F32).astype(BF)
        gu_oth_ref[...] = jnp.dot(oth_t[...], grad, preferred_element_type=F32).astype(BF)
        gb_ref[...] = jnp.sum(grad.astype(F32), 0, keepdims=True)
        gs_own_ref[...] = gs_own_ref[...] + times_rows(grad, up_own_ref[...])
        gs_oth_ref[...] = gs_oth_ref[...] + times_rows(grad, up_oth_ref[...])

    @pl.when(step < half)
    def _():
        one(down_own_ref, gd_own_ref)

    @pl.when(step >= half)
    def _():
        one(down_oth_ref, gd_oth_ref)


def feed(me, own, oth, cot, up_own, up_oth, down_own, down_oth, bias):
    tokens, half_width = own.shape
    model_width = cot.shape[1]
    ff_width = up_own.shape[1]
    z_size, block, _ = down_own.shape

    def column(j, me_ref):
        mine = me_ref[0]
        return (0, (j % z_size) * 2 + jnp.where(j < z_size, mine, 1 - mine))

    whole = lambda j, me_ref: (0, 0)
    first = lambda j, me_ref: (jnp.minimum(j, z_size - 1), 0, 0)
    second = lambda j, me_ref: (jnp.maximum(j - z_size, 0), 0, 0)
    halves = [pl.BlockSpec((tokens, half_width), whole)] * 2
    columns = [pl.BlockSpec((half_width, block), column)] * 2
    downs = [pl.BlockSpec((1, block, model_width), first), pl.BlockSpec((1, block, model_width), second)]
    line = pl.BlockSpec((1, block), column)
    all_rows = pl.BlockSpec((tokens, model_width), whole)
    return pl.pallas_call(
        feed_kernel,
        grid_spec=pltpu.PrefetchScalarGridSpec(
            num_scalar_prefetch=1,
            grid=(2 * z_size,),
            in_specs=[*halves, all_rows, *columns, *downs, line],
            out_specs=[all_rows, *halves, *downs, *columns, line],
            scratch_shapes=[pltpu.VMEM((half_width, tokens), BF)] * 2,
        ),
        out_shape=[
            jax.ShapeDtypeStruct((tokens, model_width), F32),
            jax.ShapeDtypeStruct((tokens, half_width), F32),
            jax.ShapeDtypeStruct((tokens, half_width), F32),
            jax.ShapeDtypeStruct(down_own.shape, BF),
            jax.ShapeDtypeStruct(down_own.shape, BF),
            jax.ShapeDtypeStruct(up_own.shape, BF),
            jax.ShapeDtypeStruct(up_own.shape, BF),
            jax.ShapeDtypeStruct((1, ff_width), F32),
        ],
        compiler_params=pltpu.CompilerParams(vmem_limit_bytes=VMEM_BYTES),
        cost_estimate=pl.CostEstimate(
            flops=12 * tokens * model_width * ff_width,
            bytes_accessed=8 * model_width * ff_width + 12 * tokens * model_width,
            transcendentals=tokens * ff_width,
        ),
        name="feed",
    )(me, own, oth, cot, up_own, up_oth, down_own, down_oth, bias)


def project_kernel(x_ref, gain_ref, shift_ref, w_ref, bias_ref, low_ref, q_ref, k_ref, v_ref, kt_ref, vt_ref):
    width = q_ref.shape[1]
    low = layer_norm(x_ref[...].astype(F32), gain_ref[...], shift_ref[...]).astype(BF)
    low_ref[...] = low
    made = (jnp.dot(low, w_ref[...], preferred_element_type=F32) + bias_ref[...]).astype(BF)
    made = made.astype(F32)
    keys, values = made[:, width : 2 * width], made[:, 2 * width :]
    q_ref[...] = (made[:, :width] * (HD**-0.5)).astype(BF)
    k_ref[...] = keys.astype(BF)
    v_ref[...] = values.astype(BF)
    kt_ref[...] = keys.T.astype(BF)
    vt_ref[...] = values.T.astype(BF)


def project(rows, gain, shift, weight, bias):
    length, model_width = rows.shape
    width = weight.shape[1] // 3
    block = min(512, length)
    whole = lambda i: (0, 0)
    down = lambda i: (i, 0)
    across = lambda i: (0, i)
    return pl.pallas_call(
        project_kernel,
        grid=(length // block,),
        in_specs=[
            pl.BlockSpec((block, model_width), down),
            pl.BlockSpec((1, model_width), whole),
            pl.BlockSpec((1, model_width), whole),
            pl.BlockSpec((model_width, 3 * width), whole),
            pl.BlockSpec((1, 3 * width), whole),
        ],
        out_specs=[
            pl.BlockSpec((block, model_width), down),
            pl.BlockSpec((block, width), down),
            pl.BlockSpec((block, width), down),
            pl.BlockSpec((block, width), down),
            pl.BlockSpec((width, block), across),
            pl.BlockSpec((width, block), across),
        ],
        out_shape=[jax.ShapeDtypeStruct((length, model_width), BF)]
        + [jax.ShapeDtypeStruct((length, width), BF)] * 3
        + [jax.ShapeDtypeStruct((width, length), BF)] * 2,
        compiler_params=pltpu.CompilerParams(vmem_limit_bytes=VMEM_BYTES),
        cost_estimate=pl.CostEstimate(
            flops=2 * length * model_width * 3 * width,
            bytes_accessed=4 * length * model_width + 10 * length * width,
            transcendentals=0,
        ),
        name="project",
    )(rows, gain, shift, weight, bias)


def tile_helpers(head, slope, block, width):
    lane = lax.broadcasted_iota(jnp.int32, (block, width), 1)
    mine = (lane >= head * HD) & (lane < head * HD + HD)
    key = lax.broadcasted_iota(jnp.int32, (block, block), 0)
    query = lax.broadcasted_iota(jnp.int32, (block, block), 1)
    return mine, slope * key.astype(F32), key <= query


def attend_kernel(slope_ref, q_ref, k_ref, vt_ref, o_ref, lse_ref, score_scr, out_scr):
    block, width = q_ref.shape
    number, head = pl.program_id(0), pl.program_id(1)
    slope = slope_ref[head]
    mine, bias, causal = tile_helpers(head, slope, block, width)
    queries = jnp.where(mine, q_ref[...], jnp.zeros_like(q_ref[...]))

    def one_block(last):
        highest = None
        for t in range(last + 1):
            rows = pl.ds(t * block, block)
            scores = lax.dot_general(k_ref[rows, :], queries, NT, preferred_element_type=F32) + bias
            if t == last:
                scores = jnp.where(causal, scores, -1e30)
            score_scr[rows, :] = scores
            top = jnp.max(scores, 0, keepdims=True) + slope * (t * block)
            highest = top if highest is None else jnp.maximum(highest, top)
        total = jnp.zeros((1, block), F32)
        blended = jnp.zeros((width, block), F32)
        for t in range(last + 1):
            rows = pl.ds(t * block, block)
            weights = jnp.exp(score_scr[rows, :] - (highest - slope * (t * block)))
            total = total + jnp.sum(weights, 0, keepdims=True)
            blended = blended + jnp.dot(
                vt_ref[:, rows], weights.astype(BF), preferred_element_type=F32
            )
        lse_ref[...] = (highest + jnp.log(total)).reshape(lse_ref.shape)
        result = jnp.where(mine, (blended / total).T, 0.0)

        @pl.when(head == 0)
        def _():
            out_scr[...] = result

        @pl.when(head > 0)
        def _():
            out_scr[...] = out_scr[...] + result

    for last in range(k_ref.shape[0] // block):
        pl.when(number == last)(functools.partial(one_block, last))

    @pl.when(head == pl.num_programs(1) - 1)
    def _():
        o_ref[...] = out_scr[...].astype(BF)


def attend(slopes, queries, keys, values_t):
    length, width = queries.shape
    heads = slopes.shape[0]
    block = min(256, length)
    whole = lambda i, h: (0, 0)
    down = lambda i, h: (i, 0)
    return pl.pallas_call(
        attend_kernel,
        grid=(length // block, heads),
        in_specs=[
            pl.BlockSpec(memory_space=pltpu.SMEM),
            pl.BlockSpec((block, width), down),
            pl.BlockSpec((length, width), whole),
            pl.BlockSpec((width, length), whole),
        ],
        out_specs=[
            pl.BlockSpec((block, width), down),
            pl.BlockSpec((1, 1, block), lambda i, h: (h, 0, i)),
        ],
        out_shape=[
            jax.ShapeDtypeStruct((length, width), BF),
            jax.ShapeDtypeStruct((heads, 1, length), F32),
        ],
        scratch_shapes=[pltpu.VMEM((length, block), F32), pltpu.VMEM((block, width), F32)],
        compiler_params=pltpu.CompilerParams(vmem_limit_bytes=VMEM_BYTES),
        cost_estimate=pl.CostEstimate(
            flops=8 * heads * length * length * HD,
            bytes_accessed=8 * length * width,
            transcendentals=heads * length * length // 2,
        ),
        name="attend",
    )(slopes, queries, keys, values_t)


def attend_back_kernel(
    slope_ref, q_ref, k_ref, kt_ref, v_ref, g_ref, lse_ref,
    dq_ref, dk_ref, dv_ref, prob_scr, dp_scr, dk_scr, dv_scr, dq_scr,
):
    block, width = q_ref.shape
    number, head = pl.program_id(0), pl.program_id(1)
    slope = slope_ref[head]
    mine, bias, causal = tile_helpers(head, slope, block, width)
    queries = jnp.where(mine, q_ref[...], jnp.zeros_like(q_ref[...]))
    grads = jnp.where(mine, g_ref[...], jnp.zeros_like(g_ref[...]))
    lse = lse_ref[...].reshape(1, block)

    @pl.when((number == 0) & (head == 0))
    def _():
        dk_scr[...] = jnp.zeros_like(dk_scr)
        dv_scr[...] = jnp.zeros_like(dv_scr)

    def one_block(last):
        centre = jnp.zeros((1, block), F32)
        for t in range(last + 1):
            rows = pl.ds(t * block, block)
            scores = lax.dot_general(k_ref[rows, :], queries, NT, preferred_element_type=F32) + bias
            if t == last:
                scores = jnp.where(causal, scores, -1e30)
            probs = jnp.exp(scores - (lse - slope * (t * block)))
            dp = lax.dot_general(v_ref[rows, :], grads, NT, preferred_element_type=F32)
            prob_scr[rows, :] = probs
            dp_scr[rows, :] = dp
            centre = centre + jnp.sum(probs * dp, 0, keepdims=True)
            dv_scr[rows, :] = dv_scr[rows, :] + jnp.dot(
                probs.astype(BF), grads, preferred_element_type=F32
            )
        dq = jnp.zeros((width, block), F32)
        for t in range(last + 1):
            rows = pl.ds(t * block, block)
            ds = (prob_scr[rows, :] * (dp_scr[rows, :] - centre)).astype(BF)
            dk_scr[rows, :] = dk_scr[rows, :] + jnp.dot(ds, queries, preferred_element_type=F32)
            dq = dq + jnp.dot(kt_ref[:, rows], ds, preferred_element_type=F32)
        result = jnp.where(mine, (dq * (HD**-0.5)).T, 0.0)

        @pl.when(head == 0)
        def _():
            dq_scr[...] = result

        @pl.when(head > 0)
        def _():
            dq_scr[...] = dq_scr[...] + result

    for last in range(k_ref.shape[0] // block):
        pl.when(number == last)(functools.partial(one_block, last))

    @pl.when(head == pl.num_programs(1) - 1)
    def _():
        dq_ref[...] = dq_scr[...].astype(BF)

    @pl.when((head == pl.num_programs(1) - 1) & (number == pl.num_programs(0) - 1))
    def _():
        dk_ref[...] = dk_scr[...].astype(BF)
        dv_ref[...] = dv_scr[...].astype(BF)


def attend_back(slopes, queries, keys, keys_t, values, grads, lse):
    length, width = queries.shape
    heads = slopes.shape[0]
    block = min(256, length)
    whole = lambda i, h: (0, 0)
    down = lambda i, h: (i, 0)
    return pl.pallas_call(
        attend_back_kernel,
        grid=(length // block, heads),
        in_specs=[
            pl.BlockSpec(memory_space=pltpu.SMEM),
            pl.BlockSpec((block, width), down),
            pl.BlockSpec((length, width), whole),
            pl.BlockSpec((width, length), whole),
            pl.BlockSpec((length, width), whole),
            pl.BlockSpec((block, width), down),
            pl.BlockSpec((1, 1, block), lambda i, h: (h, 0, i)),
        ],
        out_specs=[
            pl.BlockSpec((block, width), down),
            pl.BlockSpec((length, width), whole),
            pl.BlockSpec((length, width), whole),
        ],
        out_shape=[jax.ShapeDtypeStruct((length, width), BF)] * 3,
        scratch_shapes=[
            pltpu.VMEM((length, block), F32),
            pltpu.VMEM((length, block), F32),
            pltpu.VMEM((length, width), F32),
            pltpu.VMEM((length, width), F32),
            pltpu.VMEM((block, width), F32),
        ],
        compiler_params=pltpu.CompilerParams(vmem_limit_bytes=VMEM_BYTES),
        cost_estimate=pl.CostEstimate(
            flops=20 * heads * length * length * HD,
            bytes_accessed=16 * length * width,
            transcendentals=heads * length * length // 2,
        ),
        name="attend_back",
    )(slopes, queries, keys, keys_t, values, grads, lse)


def body(
    hidden_in,
    norm1_gain,
    norm1_bias,
    qkv_weight,
    qv_bias,
    alibi_slopes,
    out_weight,
    out_bias,
    norm2_gain,
    norm2_bias,
    up_weight,
    up_bias,
    down_weight,
    down_bias,
    out_grad,
):
    seq_devices = lax.axis_size(SEQ)
    fsdp_devices = lax.axis_size(FSDP)
    devices = seq_devices * fsdp_devices
    z_size, y_size, x_size = lax.axis_size("z"), lax.axis_size("fy"), lax.axis_size("fx")
    sequences, local_len, model_width = hidden_in.shape
    tokens = sequences * local_len
    heads_local = H // seq_devices
    width = heads_local * HD
    ff_width = up_weight.shape[1]
    rows_each = qkv_weight.shape[0]
    ff_each = down_weight.shape[0]
    place = lax.axis_index(SEQ)
    slopes = lax.dynamic_slice_in_dim(alibi_slopes, place * heads_local, heads_local)

    me = lax.axis_index("core")

    def split(values):
        values = values.reshape(tokens, z_size, 2, -1)
        return (
            at_index(values, me, 2).reshape(tokens, -1),
            at_index(values, 1 - me, 2).reshape(tokens, -1),
        )

    def unsplit(own, oth):
        own, oth = own.reshape(tokens, z_size, -1), oth.reshape(tokens, z_size, -1)
        return merge_pair(own, oth, "core", 2).reshape(tokens, -1)

    small_parts = (norm1_gain, norm1_bias, qv_bias, out_bias, norm2_gain, norm2_bias, up_bias, down_bias)
    small_here = jnp.concatenate(small_parts)
    small_all = lax.all_to_all(
        jnp.broadcast_to(small_here, (devices, small_here.shape[0])), ALL, split_axis=0, concat_axis=0, tiled=True
    )
    full, start = [], 0
    for part in small_parts:
        size = part.shape[0]
        full.append(small_all[:, start : start + size].reshape(-1).astype(F32))
        start += size
    first_gain, first_shift, bias_qv, b_out, second_gain, second_shift, b_up, b_down = full

    columns = qkv_weight.reshape(rows_each, 3, seq_devices, width).transpose(2, 0, 1, 3)
    columns = columns.reshape(seq_devices, rows_each, 3 * width)
    columns = lax.all_to_all(columns, SEQ, split_axis=0, concat_axis=0, tiled=True)
    w_heads = lax.all_gather(columns, FSDP, axis=1, tiled=False).reshape(model_width, 3 * width)
    bias_parts = bias_qv.reshape(2, seq_devices, width)
    bias_mine = lax.dynamic_index_in_dim(bias_parts, place, 1, keepdims=False)
    bias_heads = jnp.concatenate([bias_mine[0], jnp.zeros((width,), F32), bias_mine[1]])

    orders = (("fx", "fy"), ("fy", "fx"), ("fy", "fx"))
    along_z = [
        lax.all_gather(weight, "z", axis=0, tiled=False) for weight in (up_weight, down_weight, out_weight)
    ]
    along_z = [after(weight, w_heads, small_all) for weight in along_z]
    sent = [send_axis(w, order[0], 1) for w, order in zip(along_z, orders)]
    pairs = [join_axis(w, o, order[0], 1) for w, o, order in zip(along_z, sent, orders)]
    second_place = [1 if order[1] == "fy" else 2 for order in orders]
    sent = [send_axis(w, order[1], at) for w, order, at in zip(pairs, orders, second_place)]

    kept = []
    returned = []
    for n in range(sequences):
        rows = lax.all_gather(hidden_in[n], SEQ, axis=0, tiled=True)
        if n == sequences - 1:
            sent = [after(o, kept[0][-1]) if kept else o for o in sent]
            mine = [
                join_axis(w, o, order[1], at)
                for w, o, order, at in zip(pairs, sent, orders, second_place)
            ]
            theirs = [swap(w, "core") for w in mine]
        first_low, q, k, v, kt, vt = project(
            rows, first_gain[None], first_shift[None], w_heads, bias_heads[None]
        )
        attended, lse = attend(slopes, q, k, vt)
        returned.append(lax.all_to_all(attended, SEQ, split_axis=0, concat_axis=1, tiled=True))
        kept.append((first_low, q, k, v, kt, lse))
    attended_low = jnp.stack(returned).reshape(tokens, model_width)
    half_width = model_width // 2
    up_own, up_oth = (w.reshape(half_width, ff_width) for w in (mine[0], theirs[0]))
    down_own, down_oth = (w.reshape(z_size, -1, model_width) for w in (mine[1], theirs[1]))
    out_own, out_oth = (w.reshape(half_width, model_width) for w in (mine[2], theirs[2]))

    flat_in = hidden_in.reshape(tokens, model_width).astype(F32)
    att_own, att_oth = split(attended_low)
    middle = (
        flat_in
        + jnp.dot(att_own, out_own, preferred_element_type=F32)
        + jnp.dot(att_oth, out_oth, preferred_element_type=F32)
        + b_out
    )
    second_norm, second_back = jax.vjp(layer_norm, middle, second_gain, second_shift)
    second_own, second_oth = split(second_norm.astype(BF))
    cot_low = out_grad.reshape(tokens, model_width)
    cotangent = cot_low.astype(F32)
    y, gs_own, gs_oth, gd_own, gd_oth, gu_own, gu_oth, grad_up_bias = feed(
        me.reshape(1), second_own, second_oth, cot_low, up_own, up_oth, down_own, down_oth, b_up[None]
    )
    block_out = (middle + y + b_down).astype(BF).reshape(sequences, local_len, model_width)

    cells = (z_size, y_size, x_size)
    to_up = gu_own.reshape(*cells, rows_each, ff_width)
    to_down = gd_own.reshape(*cells, ff_each, model_width)
    sum_up = [to_up, swap(gu_oth, "core").reshape(to_up.shape)]
    sum_down = [to_down, swap(gd_oth, "core").reshape(to_down.shape)]

    grad_second = unsplit(gs_own, gs_oth)
    grad_mid_norm, grad_gain_two, grad_shift_two = second_back(grad_second)
    grad_middle = cotangent + grad_mid_norm
    grad_branch = grad_middle.astype(BF)
    grad_attended = unsplit(
        times_rows(grad_branch, out_own).astype(BF), times_rows(grad_branch, out_oth).astype(BF)
    )
    grad_attended = grad_attended.reshape(sequences, local_len, model_width)
    grad_heads = [
        lax.all_to_all(grad_attended[n], SEQ, split_axis=1, concat_axis=0, tiled=True)
        for n in range(sequences)
    ]
    go_own = outer_sum(att_own, grad_branch).astype(BF).reshape(*cells, rows_each, model_width)
    go_oth = outer_sum(att_oth, grad_branch).astype(BF)
    sum_out = [go_own, swap(go_oth, "core").reshape(go_own.shape)]
    sum_up = reduce_axis(sum_up, "fy", 1)
    sum_down = reduce_axis(sum_down, "fx", 2)
    sum_out = reduce_axis(sum_out, "fx", 2)

    rear = [
        jnp.sum(grad_branch.astype(F32), 0),
        grad_gain_two,
        grad_shift_two,
        grad_up_bias,
        jnp.sum(cotangent, 0),
    ]
    rear_wide = jnp.concatenate([part.reshape(devices, -1) for part in rear], 1)
    rear_sum = jnp.sum(lax.all_to_all(rear_wide, ALL, split_axis=0, concat_axis=0, tiled=True), 0)

    grad_qkvw = jnp.zeros((model_width, 3 * width), F32)
    column_sums = jnp.zeros((3 * width,), F32)
    grad_first = []
    for n in range(sequences):
        first_low, q, k, v, kt, lse = kept[n]
        dq, dk, dv = attend_back(slopes, q, k, kt, v, grad_heads[n], lse)
        if n == sequences - 1:
            sum_up, sum_down, sum_out = (
                terms[:-1] + [after(terms[-1], dq)] for terms in (sum_up, sum_down, sum_out)
            )
            sum_up = reduce_axis(sum_up, "fx", 1)
            sum_down = reduce_axis(sum_down, "fy", 1)
            sum_out = reduce_axis(sum_out, "fy", 1)
        grad_projected = jnp.concatenate([dq, dk, dv], 1)
        partial = times_rows(grad_projected, w_heads).astype(BF)
        grad_first.append(lax.psum_scatter(partial, SEQ, scatter_dimension=0, tiled=True))
        grad_qkvw = grad_qkvw + outer_sum(first_low, grad_projected)
        column_sums = column_sums + jnp.sum(grad_projected.astype(F32), 0)

    wide = [grad_qkvw.reshape(seq_devices, y_size, x_size, rows_each, 3 * width)]
    wide = total_of(reduce_axis(reduce_axis(wide, "fy", 1), "fx", 1))
    wide = lax.all_to_all(wide, SEQ, split_axis=0, concat_axis=0, tiled=True)
    wide = wide.reshape(seq_devices, rows_each, 3, width).transpose(1, 2, 0, 3)
    out_qkvw = wide.reshape(rows_each, 3 * model_width)

    low_sum = jnp.concatenate([total_of(sum_out).astype(BF), total_of(sum_down).astype(BF)], 1)
    low_sum = lax.psum_scatter(low_sum, "z", scatter_dimension=0, tiled=False).astype(F32)
    out_outw, out_down = low_sum[:rows_each], low_sum[rows_each:]
    out_up = total_of(sum_up).astype(BF)
    out_up = lax.psum_scatter(out_up, "z", scatter_dimension=0, tiled=False).astype(F32)

    grad_first = jnp.stack(grad_first).reshape(tokens, model_width).astype(F32)
    _, first_back = jax.vjp(layer_norm, flat_in, first_gain, first_shift)
    grad_in_norm, grad_gain_one, grad_shift_one = first_back(grad_first)
    input_grad = (grad_middle + grad_in_norm).reshape(sequences, local_len, model_width)

    qv_here = jnp.zeros((2, seq_devices, width), F32)
    qv_mine = jnp.stack([column_sums[:width], column_sums[2 * width :]])
    qv_here = lax.dynamic_update_slice_in_dim(qv_here, qv_mine[:, None], place, 1)
    front = [grad_gain_one, grad_shift_one, qv_here.reshape(-1)]
    front_wide = jnp.concatenate([part.reshape(devices, -1) for part in front], 1)
    front_sum = jnp.sum(lax.all_to_all(front_wide, ALL, split_axis=0, concat_axis=0, tiled=True), 0)

    r = rows_each
    return (
        block_out,
        input_grad,
        front_sum[:r],
        front_sum[r : 2 * r],
        out_qkvw,
        front_sum[2 * r :],
        out_outw,
        rear_sum[:r],
        rear_sum[r : 2 * r],
        rear_sum[2 * r : 3 * r],
        out_up,
        rear_sum[3 * r : 3 * r + ff_each],
        out_down,
        rear_sum[3 * r + ff_each :],
    )


def solution(mesh):
    seq_size, fsdp_size = mesh.shape["seq"], mesh.shape["fsdp"]
    fine = Mesh(mesh.devices.reshape(seq_size // 2, 2, fsdp_size // 2, 2), ALL)
    tokens = P(FSDP, SEQ, None)
    vector = P(ALL)
    matrix = P(ALL, None)
    return jax.shard_map(
        body,
        mesh=fine,
        in_specs=(
            tokens, vector, vector, matrix, vector, P(), matrix, vector, vector, vector,
            matrix, vector, matrix, vector, tokens,
        ),
        out_specs=(
            tokens, tokens, vector, vector, matrix, vector, matrix, vector, vector, vector,
            matrix, vector, matrix, vector,
        ),
        check_vma=False,
    )
```

```python
import functools

import jax
import jax.numpy as jnp
from jax import lax
from jax.experimental import pallas as pl
from jax.experimental.pallas import tpu as pltpu
from jax.sharding import Mesh
from jax.sharding import PartitionSpec as P

H = 16
HD = 64
SEQ = ("z", "core")
FSDP = ("fy", "fx")
ALL = SEQ + FSDP
BF = jnp.bfloat16
F32 = jnp.float32
NT = (((1,), (1,)), ((), ()))
VMEM_BYTES = 48 * 1024 * 1024
LIGHT = pl.CostEstimate(flops=1024, bytes_accessed=1024, transcendentals=0)


def layer_norm(values, norm_gain, norm_shift):
    average = jnp.mean(values, -1, keepdims=True)
    centered = values - average
    variance = jnp.mean(centered * centered, -1, keepdims=True)
    return centered * lax.rsqrt(variance + 1e-05) * norm_gain + norm_shift


def outer_sum(left, right):
    return lax.dot_general(left, right, (((0,), (0,)), ((), ())), preferred_element_type=F32)


def times_rows(left, right):
    return lax.dot_general(left, right, NT, preferred_element_type=F32)


def swap(values, axis):
    return lax.ppermute(values, axis, [(0, 1), (1, 0)])


def after(values, *earlier):
    return lax.optimization_barrier((values, *earlier))[0]


def merge_pair(mine, other, axis, position):
    shape = [1] * (mine.ndim + 1)
    shape[position] = 2
    slot = jnp.arange(2).reshape(shape)
    return jnp.where(
        slot == lax.axis_index(axis), jnp.expand_dims(mine, position), jnp.expand_dims(other, position)
    )


def line_gather(values, axis, *earlier):
    size, me = lax.axis_size(axis), lax.axis_index(axis)
    held = jnp.zeros((3 * size - 2, *values.shape), values.dtype)
    held = lax.dynamic_update_index_in_dim(held, values, me + size - 1, 0)
    up = down = values
    for step in range(1, size):
        if step == size - 1:
            up, down = after(up, *earlier), after(down, *earlier)
        up = lax.ppermute(up, axis, [(i - 1, i) for i in range(step, size)])
        down = lax.ppermute(down, axis, [(i + 1, i) for i in range(size - step)])
        held = lax.dynamic_update_index_in_dim(held, up, me - step + size - 1, 0)
        held = lax.dynamic_update_index_in_dim(held, down, me + step + size - 1, 0)
    return held[size - 1 : 2 * size - 1]


def line_reduce(values, axis):
    size, me = lax.axis_size(axis), lax.axis_index(axis)
    up = down = 0.0
    for step in range(1, size):
        above = jnp.minimum(me + size - step, size - 1)
        below = jnp.maximum(me - size + step, 0)
        up = (at_index(values, above, 0).astype(F32) + up).astype(BF)
        down = (at_index(values, below, 0).astype(F32) + down).astype(BF)
        up = lax.ppermute(up, axis, [(i, i + 1) for i in range(step)]).astype(F32)
        down = lax.ppermute(down, axis, [(i, i - 1) for i in range(size - step, size)]).astype(F32)
    return at_index(values, me, 0).astype(F32) + up + down


def send_axis(values, axis, position):
    if lax.axis_size(axis) != 2:
        return lax.all_gather(values, axis, axis=position, tiled=False)
    return swap(values, axis)


def join_axis(values, other, axis, position):
    if lax.axis_size(axis) != 2:
        return other
    return merge_pair(values, other, axis, position)


def at_index(values, index, position):
    return lax.dynamic_index_in_dim(values, index, position, keepdims=False)


def total_of(terms):
    total = terms[0].astype(F32)
    for term in terms[1:]:
        total = total + term.astype(F32)
    return total


def give_part(terms, axis, position):
    if lax.axis_size(axis) != 2:
        return total_of(terms).astype(BF)
    other = 1 - lax.axis_index(axis)
    return total_of([at_index(term, other, position) for term in terms]).astype(BF)


def take_part(terms, given, axis, position):
    if lax.axis_size(axis) != 2:
        return [lax.psum_scatter(given, axis, scatter_dimension=position, tiled=False)]
    me = lax.axis_index(axis)
    return [at_index(term, me, position) for term in terms] + [swap(given, axis)]


def reduce_axis(terms, axis, position):
    return take_part(terms, give_part(terms, axis, position), axis, position)


def normalize(values):
    average = jnp.mean(values, -1, keepdims=True)
    centered = values - average
    variance = jnp.mean(centered * centered, -1, keepdims=True)
    scale = lax.rsqrt(variance + 1e-05)
    return centered * scale, scale


def norm_back(grad, normal, scale, gain):
    scaled = grad * gain
    inner = jnp.mean(scaled * normal, -1, keepdims=True)
    return scale * (scaled - jnp.mean(scaled, -1, keepdims=True) - normal * inner)


def branch_kernel(
    me_ref, att_ref, x_ref, w_own_ref, w_oth_ref, bias_ref, gain_ref, shift_ref, middle_ref, own_ref, oth_ref
):
    me = me_ref[0]
    z_size, block, _ = w_own_ref.shape
    middle = x_ref[...].astype(F32) + bias_ref[...]
    for z in range(z_size):
        middle = middle + jnp.dot(att_ref[2 * z + me], w_own_ref[z], preferred_element_type=F32)
        middle = middle + jnp.dot(att_ref[2 * z + 1 - me], w_oth_ref[z], preferred_element_type=F32)
    middle_ref[...] = middle
    normal, _ = normalize(middle)
    normal = normal * gain_ref[...] + shift_ref[...]
    for z in range(z_size):
        even = normal[:, 2 * z * block : (2 * z + 1) * block]
        odd = normal[:, (2 * z + 1) * block : (2 * z + 2) * block]
        own_ref[:, z * block : (z + 1) * block] = jnp.where(me == 0, even, odd).astype(BF)
        oth_ref[:, z * block : (z + 1) * block] = jnp.where(me == 0, odd, even).astype(BF)


def branch(me, att, rows, w_own, w_oth, bias, gain, shift):
    length, model_width = rows.shape
    vmem = pl.BlockSpec(memory_space=pltpu.VMEM)
    return pl.pallas_call(
        branch_kernel,
        in_specs=[pl.BlockSpec(memory_space=pltpu.SMEM)] + [vmem] * 7,
        out_specs=[vmem] * 3,
        out_shape=[
            jax.ShapeDtypeStruct((length, model_width), F32),
            jax.ShapeDtypeStruct((length, model_width // 2), BF),
            jax.ShapeDtypeStruct((length, model_width // 2), BF),
        ],
        compiler_params=pltpu.CompilerParams(vmem_limit_bytes=VMEM_BYTES),
        cost_estimate=LIGHT,
        name="branch",
    )(me, att, rows, w_own, w_oth, bias, gain, shift)


def middle_back_kernel(
    me_ref, gs_own_ref, gs_oth_ref, middle_ref, cot_ref, y_ref, bias_ref, gain_ref, w_own_ref, w_oth_ref, *rest
):
    gm_ref, gb_ref, ga_ref, sums_ref, out_ref, grad_scr = rest[-6:]
    me = me_ref[0]
    z_size, block, _ = w_own_ref.shape
    for z in range(z_size):
        own = gs_own_ref[:, z * block : (z + 1) * block]
        oth = gs_oth_ref[:, z * block : (z + 1) * block]
        grad_scr[:, 2 * z * block : (2 * z + 1) * block] = jnp.where(me == 0, own, oth)
        grad_scr[:, (2 * z + 1) * block : (2 * z + 2) * block] = jnp.where(me == 0, oth, own)
    middle = middle_ref[...]
    out_ref[0] = (middle + y_ref[...] + bias_ref[...]).astype(BF)
    normal, scale = normalize(middle)
    grad = grad_scr[...]
    cot = cot_ref[...].astype(F32)
    grad_middle = cot + norm_back(grad, normal, scale, gain_ref[...])
    gm_ref[...] = grad_middle
    low = grad_middle.astype(BF)
    gb_ref[...] = low
    for z in range(z_size):
        ga_ref[2 * z + me] = times_rows(low, w_own_ref[z]).astype(BF)
        ga_ref[2 * z + 1 - me] = times_rows(low, w_oth_ref[z]).astype(BF)
    sums_ref[0:1, :] = jnp.sum(low.astype(F32), 0, keepdims=True)
    sums_ref[1:2, :] = jnp.sum(grad * normal, 0, keepdims=True)
    sums_ref[2:3, :] = jnp.sum(grad, 0, keepdims=True)
    sums_ref[3:4, :] = jnp.sum(cot, 0, keepdims=True)


def middle_back(n, sequences, me, gs_own, gs_oth, middle, cot, y, bias, gain, w_own, w_oth, filled):
    length, model_width = middle.shape
    z_size, block, _ = w_own.shape
    whole = lambda i: (0, 0)
    part = lambda i: (n, 0)
    cube = lambda i: (0, 0, 0)
    half = pl.BlockSpec((length, model_width // 2), part)
    line = pl.BlockSpec((1, model_width), whole)
    matrix = pl.BlockSpec(w_own.shape, cube)
    full = pl.BlockSpec((length, model_width), whole)
    extra = [] if filled is None else [filled]
    return pl.pallas_call(
        middle_back_kernel,
        grid=(1,),
        in_specs=[
            pl.BlockSpec(memory_space=pltpu.SMEM), half, half, full, full,
            pl.BlockSpec((length, model_width), part), line, line, matrix, matrix,
        ]
        + [pl.BlockSpec(memory_space=pl.ANY)] * len(extra),
        out_specs=[
            full,
            full,
            pl.BlockSpec((2 * z_size, length, block), cube),
            pl.BlockSpec((8, model_width), whole),
            pl.BlockSpec((1, length, model_width), lambda i: (n, 0, 0)),
        ],
        out_shape=[
            jax.ShapeDtypeStruct((length, model_width), F32),
            jax.ShapeDtypeStruct((length, model_width), BF),
            jax.ShapeDtypeStruct((2 * z_size, length, block), BF),
            jax.ShapeDtypeStruct((8, model_width), F32),
            jax.ShapeDtypeStruct((sequences, length, model_width), BF),
        ],
        scratch_shapes=[pltpu.VMEM((length, model_width), F32)],
        input_output_aliases={10: 4} if extra else {},
        compiler_params=pltpu.CompilerParams(vmem_limit_bytes=VMEM_BYTES),
        cost_estimate=LIGHT,
        name="middle_back",
    )(me, gs_own, gs_oth, middle, cot, y, bias, gain, w_own, w_oth, *extra)


def out_weight_kernel(sequences, me_ref, *refs):
    own_refs, oth_refs = refs[:sequences], refs[sequences : 2 * sequences]
    grad_refs = refs[2 * sequences : 3 * sequences]
    go_own_ref, go_oth_ref = refs[3 * sequences :]
    for att_refs, out_ref in ((own_refs, go_own_ref), (oth_refs, go_oth_ref)):
        total = outer_sum(att_refs[0][0], grad_refs[0][...])
        for att_ref, grad_ref in zip(att_refs[1:], grad_refs[1:]):
            total = total + outer_sum(att_ref[0], grad_ref[...])
        out_ref[0] = total.astype(BF)


def out_weight_grad(me, atts, grads):
    sequences = len(atts)
    devices, length, block = atts[0].shape
    model_width = grads[0].shape[1]
    z_size = devices // 2
    own = pl.BlockSpec((1, length, block), lambda z, me_ref: (2 * z + me_ref[0], 0, 0))
    oth = pl.BlockSpec((1, length, block), lambda z, me_ref: (2 * z + 1 - me_ref[0], 0, 0))
    full = pl.BlockSpec((length, model_width), lambda z, me_ref: (0, 0))
    out = pl.BlockSpec((1, block, model_width), lambda z, me_ref: (z, 0, 0))
    shape = jax.ShapeDtypeStruct((z_size, block, model_width), BF)
    return pl.pallas_call(
        functools.partial(out_weight_kernel, sequences),
        grid_spec=pltpu.PrefetchScalarGridSpec(
            num_scalar_prefetch=1,
            grid=(z_size,),
            in_specs=[own] * sequences + [oth] * sequences + [full] * sequences,
            out_specs=[out, out],
        ),
        out_shape=[shape, shape],
        compiler_params=pltpu.CompilerParams(vmem_limit_bytes=VMEM_BYTES),
        cost_estimate=LIGHT,
        name="out_weight_grad",
    )(me, *atts, *atts, *grads)


def first_back_kernel(grad_ref, x_ref, gain_ref, gm_ref, *rest):
    sums_ref, out_ref = rest[-2:]
    grad = grad_ref[...].astype(F32)
    normal, scale = normalize(x_ref[...].astype(F32))
    out_ref[0] = gm_ref[...] + norm_back(grad, normal, scale, gain_ref[...])
    sums_ref[0:1, :] = jnp.sum(grad * normal, 0, keepdims=True)
    sums_ref[1:2, :] = jnp.sum(grad, 0, keepdims=True)


def first_back(n, sequences, grad, rows, gain, grad_middle, filled):
    length, model_width = rows.shape
    whole = lambda i: (0, 0)
    full = pl.BlockSpec((length, model_width), whole)
    extra = [] if filled is None else [filled]
    return pl.pallas_call(
        first_back_kernel,
        grid=(1,),
        in_specs=[full, full, pl.BlockSpec((1, model_width), whole), full]
        + [pl.BlockSpec(memory_space=pl.ANY)] * len(extra),
        out_specs=[
            pl.BlockSpec((8, model_width), whole),
            pl.BlockSpec((1, length, model_width), lambda i: (n, 0, 0)),
        ],
        out_shape=[
            jax.ShapeDtypeStruct((8, model_width), F32),
            jax.ShapeDtypeStruct((sequences, length, model_width), F32),
        ],
        input_output_aliases={4: 1} if extra else {},
        compiler_params=pltpu.CompilerParams(vmem_limit_bytes=VMEM_BYTES),
        cost_estimate=LIGHT,
        name="first_back",
    )(grad, rows, gain, grad_middle, *extra)


def feed_kernel(sequences, me_ref, *refs):
    own_refs, oth_refs, refs = refs[:sequences], refs[sequences : 2 * sequences], refs[2 * sequences :]
    cot_ref, up_own_ref, up_oth_ref, down_own_ref, down_oth_ref, bias_ref = refs[:6]
    y_ref, gs_own_ref, gs_oth_ref, gd_own_ref, gd_oth_ref, gu_own_ref, gu_oth_ref, gb_ref = refs[6:14]
    own_ref, oth_ref, own_t, oth_t = refs[14:]
    step = pl.program_id(0)
    half = pl.num_programs(0) // 2
    length = own_refs[0].shape[0]

    @pl.when(step == 0)
    def _():
        for n in range(sequences):
            own_ref[n * length : (n + 1) * length, :] = own_refs[n][...]
            oth_ref[n * length : (n + 1) * length, :] = oth_refs[n][...]
        own_t[...] = own_ref[...].astype(F32).T.astype(BF)
        oth_t[...] = oth_ref[...].astype(F32).T.astype(BF)
        y_ref[...] = jnp.zeros_like(y_ref)
        gs_own_ref[...] = jnp.zeros_like(gs_own_ref)
        gs_oth_ref[...] = jnp.zeros_like(gs_oth_ref)

    def one(down_ref, gd_ref):
        down = down_ref[0]
        pre = jnp.dot(own_ref[...], up_own_ref[...], preferred_element_type=F32)
        pre = pre + jnp.dot(oth_ref[...], up_oth_ref[...], preferred_element_type=F32)
        pre = pre + bias_ref[...]
        square = pre * pre
        tanh = jnp.tanh(0.7978845608 * (pre + 0.044715 * pre * square))
        near = 0.5 * (1.0 + tanh)
        active = (pre * near).astype(BF)
        slope = near + 0.5 * pre * (1.0 - tanh * tanh) * (
            0.7978845608 * (1.0 + 3.0 * 0.044715 * square)
        )
        grad = lax.dot_general(cot_ref[...], down, NT, preferred_element_type=F32) * slope
        grad = grad.astype(BF)
        y_ref[...] = y_ref[...] + jnp.dot(active, down, preferred_element_type=F32)
        gd_ref[0] = outer_sum(active, cot_ref[...]).astype(BF)
        gu_own_ref[...] = jnp.dot(own_t[...], grad, preferred_element_type=F32).astype(BF)
        gu_oth_ref[...] = jnp.dot(oth_t[...], grad, preferred_element_type=F32).astype(BF)
        gb_ref[...] = jnp.sum(grad.astype(F32), 0, keepdims=True)
        gs_own_ref[...] = gs_own_ref[...] + times_rows(grad, up_own_ref[...])
        gs_oth_ref[...] = gs_oth_ref[...] + times_rows(grad, up_oth_ref[...])

    @pl.when(step < half)
    def _():
        one(down_own_ref, gd_own_ref)

    @pl.when(step >= half)
    def _():
        one(down_oth_ref, gd_oth_ref)


def feed(me, owns, oths, cot, up_own, up_oth, down_own, down_oth, bias):
    sequences = len(owns)
    length, half_width = owns[0].shape
    tokens, model_width = cot.shape
    ff_width = up_own.shape[1]
    z_size, block, _ = down_own.shape

    def column(j, me_ref):
        mine = me_ref[0]
        return (0, (j % z_size) * 2 + jnp.where(j < z_size, mine, 1 - mine))

    whole = lambda j, me_ref: (0, 0)
    first = lambda j, me_ref: (jnp.minimum(j, z_size - 1), 0, 0)
    second = lambda j, me_ref: (jnp.maximum(j - z_size, 0), 0, 0)
    halves = [pl.BlockSpec((tokens, half_width), whole)] * 2
    pieces = [pl.BlockSpec((length, half_width), whole)] * (2 * sequences)
    columns = [pl.BlockSpec((half_width, block), column)] * 2
    downs = [pl.BlockSpec((1, block, model_width), first), pl.BlockSpec((1, block, model_width), second)]
    line = pl.BlockSpec((1, block), column)
    all_rows = pl.BlockSpec((tokens, model_width), whole)
    return pl.pallas_call(
        functools.partial(feed_kernel, sequences),
        grid_spec=pltpu.PrefetchScalarGridSpec(
            num_scalar_prefetch=1,
            grid=(2 * z_size,),
            in_specs=[*pieces, all_rows, *columns, *downs, line],
            out_specs=[all_rows, *halves, *downs, *columns, line],
            scratch_shapes=[pltpu.VMEM((tokens, half_width), BF)] * 2
            + [pltpu.VMEM((half_width, tokens), BF)] * 2,
        ),
        out_shape=[
            jax.ShapeDtypeStruct((tokens, model_width), F32),
            jax.ShapeDtypeStruct((tokens, half_width), F32),
            jax.ShapeDtypeStruct((tokens, half_width), F32),
            jax.ShapeDtypeStruct(down_own.shape, BF),
            jax.ShapeDtypeStruct(down_own.shape, BF),
            jax.ShapeDtypeStruct(up_own.shape, BF),
            jax.ShapeDtypeStruct(up_own.shape, BF),
            jax.ShapeDtypeStruct((1, ff_width), F32),
        ],
        compiler_params=pltpu.CompilerParams(vmem_limit_bytes=VMEM_BYTES),
        cost_estimate=LIGHT,
        name="feed",
    )(me, *owns, *oths, cot, up_own, up_oth, down_own, down_oth, bias)


def project_kernel(x_ref, gain_ref, shift_ref, w_ref, bias_ref, low_ref, q_ref, k_ref, v_ref, kt_ref, vt_ref):
    width = q_ref.shape[1]
    low = layer_norm(x_ref[...].astype(F32), gain_ref[...], shift_ref[...]).astype(BF)
    low_ref[...] = low
    made = (jnp.dot(low, w_ref[...], preferred_element_type=F32) + bias_ref[...]).astype(BF)
    made = made.astype(F32)
    keys, values = made[:, width : 2 * width], made[:, 2 * width :]
    q_ref[...] = (made[:, :width] * (HD**-0.5)).astype(BF)
    k_ref[...] = keys.astype(BF)
    v_ref[...] = values.astype(BF)
    kt_ref[...] = keys.T.astype(BF)
    vt_ref[...] = values.T.astype(BF)


def project(rows, gain, shift, weight, bias):
    length, model_width = rows.shape
    width = weight.shape[1] // 3
    block = min(512, length)
    whole = lambda i: (0, 0)
    down = lambda i: (i, 0)
    across = lambda i: (0, i)
    return pl.pallas_call(
        project_kernel,
        grid=(length // block,),
        in_specs=[
            pl.BlockSpec((block, model_width), down),
            pl.BlockSpec((1, model_width), whole),
            pl.BlockSpec((1, model_width), whole),
            pl.BlockSpec((model_width, 3 * width), whole),
            pl.BlockSpec((1, 3 * width), whole),
        ],
        out_specs=[
            pl.BlockSpec((block, model_width), down),
            pl.BlockSpec((block, width), down),
            pl.BlockSpec((block, width), down),
            pl.BlockSpec((block, width), down),
            pl.BlockSpec((width, block), across),
            pl.BlockSpec((width, block), across),
        ],
        out_shape=[jax.ShapeDtypeStruct((length, model_width), BF)]
        + [jax.ShapeDtypeStruct((length, width), BF)] * 3
        + [jax.ShapeDtypeStruct((width, length), BF)] * 2,
        compiler_params=pltpu.CompilerParams(vmem_limit_bytes=VMEM_BYTES),
        cost_estimate=LIGHT,
        name="project",
    )(rows, gain, shift, weight, bias)


def tile_helpers(head, slope, block, width):
    lane = lax.broadcasted_iota(jnp.int32, (block, width), 1)
    mine = (lane >= head * HD) & (lane < head * HD + HD)
    key = lax.broadcasted_iota(jnp.int32, (block, block), 0)
    query = lax.broadcasted_iota(jnp.int32, (block, block), 1)
    return mine, slope * key.astype(F32), key <= query


def attend_kernel(slope_ref, q_ref, k_ref, vt_ref, o_ref, lse_ref, score_scr, out_scr):
    block, width = q_ref.shape
    number, head = pl.program_id(0), pl.program_id(1)
    slope = slope_ref[head]
    mine, bias, causal = tile_helpers(head, slope, block, width)
    queries = jnp.where(mine, q_ref[...], jnp.zeros_like(q_ref[...]))

    def one_block(last):
        highest = None
        for t in range(last + 1):
            rows = pl.ds(t * block, block)
            scores = lax.dot_general(k_ref[rows, :], queries, NT, preferred_element_type=F32) + bias
            if t == last:
                scores = jnp.where(causal, scores, -1e30)
            score_scr[rows, :] = scores
            top = jnp.max(scores, 0, keepdims=True) + slope * (t * block)
            highest = top if highest is None else jnp.maximum(highest, top)
        total = jnp.zeros((1, block), F32)
        blended = jnp.zeros((width, block), F32)
        for t in range(last + 1):
            rows = pl.ds(t * block, block)
            weights = jnp.exp(score_scr[rows, :] - (highest - slope * (t * block)))
            total = total + jnp.sum(weights, 0, keepdims=True)
            blended = blended + jnp.dot(
                vt_ref[:, rows], weights.astype(BF), preferred_element_type=F32
            )
        lse_ref[...] = (highest + jnp.log(total)).reshape(lse_ref.shape)
        result = jnp.where(mine, (blended / total).T, 0.0)

        @pl.when(head == 0)
        def _():
            out_scr[...] = result

        @pl.when(head > 0)
        def _():
            out_scr[...] = out_scr[...] + result

    for last in range(k_ref.shape[0] // block):
        pl.when(number == last)(functools.partial(one_block, last))

    @pl.when(head == pl.num_programs(1) - 1)
    def _():
        o_ref[...] = out_scr[...].astype(BF)


def attend(slopes, queries, keys, values_t):
    length, width = queries.shape
    heads = slopes.shape[0]
    block = min(256, length)
    whole = lambda i, h: (0, 0)
    down = lambda i, h: (i, 0)
    return pl.pallas_call(
        attend_kernel,
        grid=(length // block, heads),
        in_specs=[
            pl.BlockSpec(memory_space=pltpu.SMEM),
            pl.BlockSpec((block, width), down),
            pl.BlockSpec((length, width), whole),
            pl.BlockSpec((width, length), whole),
        ],
        out_specs=[
            pl.BlockSpec((block, width), down),
            pl.BlockSpec((1, 1, block), lambda i, h: (h, 0, i)),
        ],
        out_shape=[
            jax.ShapeDtypeStruct((length, width), BF),
            jax.ShapeDtypeStruct((heads, 1, length), F32),
        ],
        scratch_shapes=[pltpu.VMEM((length, block), F32), pltpu.VMEM((block, width), F32)],
        compiler_params=pltpu.CompilerParams(vmem_limit_bytes=VMEM_BYTES),
        cost_estimate=LIGHT,
        name="attend",
    )(slopes, queries, keys, values_t)


def attend_back_kernel(
    slope_ref, q_ref, k_ref, kt_ref, v_ref, g_ref, lse_ref,
    dq_ref, dk_ref, dv_ref, prob_scr, dp_scr, dk_scr, dv_scr, dq_scr,
):
    block, width = q_ref.shape
    number, head = pl.program_id(0), pl.program_id(1)
    slope = slope_ref[head]
    mine, bias, causal = tile_helpers(head, slope, block, width)
    queries = jnp.where(mine, q_ref[...], jnp.zeros_like(q_ref[...]))
    grads = jnp.where(mine, g_ref[...], jnp.zeros_like(g_ref[...]))
    lse = lse_ref[...].reshape(1, block)

    @pl.when((number == 0) & (head == 0))
    def _():
        dk_scr[...] = jnp.zeros_like(dk_scr)
        dv_scr[...] = jnp.zeros_like(dv_scr)

    def one_block(last):
        centre = jnp.zeros((1, block), F32)
        for t in range(last + 1):
            rows = pl.ds(t * block, block)
            scores = lax.dot_general(k_ref[rows, :], queries, NT, preferred_element_type=F32) + bias
            if t == last:
                scores = jnp.where(causal, scores, -1e30)
            probs = jnp.exp(scores - (lse - slope * (t * block)))
            dp = lax.dot_general(v_ref[rows, :], grads, NT, preferred_element_type=F32)
            prob_scr[rows, :] = probs
            dp_scr[rows, :] = dp
            centre = centre + jnp.sum(probs * dp, 0, keepdims=True)
            dv_scr[rows, :] = dv_scr[rows, :] + jnp.dot(
                probs.astype(BF), grads, preferred_element_type=F32
            )
        dq = jnp.zeros((width, block), F32)
        for t in range(last + 1):
            rows = pl.ds(t * block, block)
            ds = (prob_scr[rows, :] * (dp_scr[rows, :] - centre)).astype(BF)
            dk_scr[rows, :] = dk_scr[rows, :] + jnp.dot(ds, queries, preferred_element_type=F32)
            dq = dq + jnp.dot(kt_ref[:, rows], ds, preferred_element_type=F32)
        result = jnp.where(mine, (dq * (HD**-0.5)).T, 0.0)

        @pl.when(head == 0)
        def _():
            dq_scr[...] = result

        @pl.when(head > 0)
        def _():
            dq_scr[...] = dq_scr[...] + result

    for last in range(k_ref.shape[0] // block):
        pl.when(number == last)(functools.partial(one_block, last))

    @pl.when(head == pl.num_programs(1) - 1)
    def _():
        dq_ref[...] = dq_scr[...].astype(BF)

    @pl.when((head == pl.num_programs(1) - 1) & (number == pl.num_programs(0) - 1))
    def _():
        dk_ref[...] = dk_scr[...].astype(BF)
        dv_ref[...] = dv_scr[...].astype(BF)


def attend_back(slopes, queries, keys, keys_t, values, grads, lse):
    length, width = queries.shape
    heads = slopes.shape[0]
    block = min(256, length)
    whole = lambda i, h: (0, 0)
    down = lambda i, h: (i, 0)
    return pl.pallas_call(
        attend_back_kernel,
        grid=(length // block, heads),
        in_specs=[
            pl.BlockSpec(memory_space=pltpu.SMEM),
            pl.BlockSpec((block, width), down),
            pl.BlockSpec((length, width), whole),
            pl.BlockSpec((width, length), whole),
            pl.BlockSpec((length, width), whole),
            pl.BlockSpec((block, width), down),
            pl.BlockSpec((1, 1, block), lambda i, h: (h, 0, i)),
        ],
        out_specs=[
            pl.BlockSpec((block, width), down),
            pl.BlockSpec((length, width), whole),
            pl.BlockSpec((length, width), whole),
        ],
        out_shape=[jax.ShapeDtypeStruct((length, width), BF)] * 3,
        scratch_shapes=[
            pltpu.VMEM((length, block), F32),
            pltpu.VMEM((length, block), F32),
            pltpu.VMEM((length, width), F32),
            pltpu.VMEM((length, width), F32),
            pltpu.VMEM((block, width), F32),
        ],
        compiler_params=pltpu.CompilerParams(vmem_limit_bytes=VMEM_BYTES),
        cost_estimate=LIGHT,
        name="attend_back",
    )(slopes, queries, keys, keys_t, values, grads, lse)


def body(
    hidden_in,
    norm1_gain,
    norm1_bias,
    qkv_weight,
    qv_bias,
    alibi_slopes,
    out_weight,
    out_bias,
    norm2_gain,
    norm2_bias,
    up_weight,
    up_bias,
    down_weight,
    down_bias,
    out_grad,
):
    seq_devices = lax.axis_size(SEQ)
    fsdp_devices = lax.axis_size(FSDP)
    devices = seq_devices * fsdp_devices
    z_size, y_size, x_size = lax.axis_size("z"), lax.axis_size("fy"), lax.axis_size("fx")
    sequences, local_len, model_width = hidden_in.shape
    tokens = sequences * local_len
    heads_local = H // seq_devices
    width = heads_local * HD
    ff_width = up_weight.shape[1]
    rows_each = qkv_weight.shape[0]
    ff_each = down_weight.shape[0]
    place = lax.axis_index(SEQ)
    slopes = lax.dynamic_slice_in_dim(alibi_slopes, place * heads_local, heads_local)

    me = lax.axis_index("core")

    small_parts = (norm1_gain, norm1_bias, qv_bias, out_bias, norm2_gain, norm2_bias, up_bias, down_bias)
    small_here = jnp.concatenate(small_parts)
    small_all = lax.all_to_all(
        jnp.broadcast_to(small_here, (devices, small_here.shape[0])), ALL, split_axis=0, concat_axis=0, tiled=True
    )
    full, start = [], 0
    for part in small_parts:
        size = part.shape[0]
        full.append(small_all[:, start : start + size].reshape(-1).astype(F32))
        start += size
    first_gain, first_shift, bias_qv, b_out, second_gain, second_shift, b_up, b_down = full

    columns = qkv_weight.reshape(rows_each, 3, seq_devices, width).transpose(2, 0, 1, 3)
    columns = columns.reshape(seq_devices, rows_each, 3 * width)
    columns = lax.all_to_all(columns, SEQ, split_axis=0, concat_axis=0, tiled=True)
    w_heads = lax.all_gather(columns, FSDP, axis=1, tiled=False).reshape(model_width, 3 * width)
    bias_parts = bias_qv.reshape(2, seq_devices, width)
    bias_mine = lax.dynamic_index_in_dim(bias_parts, place, 1, keepdims=False)
    bias_heads = jnp.concatenate([bias_mine[0], jnp.zeros((width,), F32), bias_mine[1]])

    low_z = lax.all_gather(jnp.concatenate([out_weight, down_weight], 0), "z", axis=0, tiled=False)
    low_z = after(low_z, small_all)
    down_z, out_z = low_z[:, rows_each:], low_z[:, :rows_each]
    down_sent, out_sent = send_axis(down_z, "fy", 1), send_axis(out_z, "fy", 1)
    down_pair = join_axis(down_z, down_sent, "fy", 1)
    out_pair = join_axis(out_z, out_sent, "fy", 1)
    up_z = line_gather(after(up_weight, columns), "z", down_pair, out_pair, w_heads)
    up_sent = send_axis(up_z, "fx", 1)
    down_sent, out_sent = send_axis(down_pair, "fx", 2), send_axis(out_pair, "fx", 2)

    kept = []
    returned = []
    ahead = (up_z, down_pair, out_pair)
    for n in range(sequences):
        rows = after(lax.all_gather(hidden_in[n], SEQ, axis=0, tiled=True), *ahead)
        first_low, q, k, v, kt, vt = project(
            rows, first_gain[None], first_shift[None], w_heads, bias_heads[None]
        )
        attended, lse = attend(slopes, q, k, vt)
        attended = attended.reshape(seq_devices, local_len, width)
        returned.append(lax.all_to_all(attended, SEQ, split_axis=0, concat_axis=0, tiled=True))
        kept.append((first_low, q, k, v, kt, lse))
        ahead = (returned[n],)
        if n == 0:
            up_sent, down_sent, out_sent, _ = lax.optimization_barrier(
                (up_sent, down_sent, out_sent, lse)
            )
            up_pair = join_axis(up_z, up_sent, "fx", 1)
            up_sent = send_axis(up_pair, "fy", 1)
            down_own = join_axis(down_pair, after(down_sent, up_pair), "fx", 2)
            out_own = join_axis(out_pair, after(out_sent, up_pair), "fx", 2)
            down_oth, out_oth = swap(down_own, "core"), swap(out_own, "core")
            ahead = (*ahead, up_pair, down_own, out_own)
    up_own = join_axis(up_pair, after(up_sent, lse), "fy", 1)
    up_oth = swap(up_own, "core")
    half_width = model_width // 2
    up_own, up_oth = (w.reshape(half_width, ff_width) for w in (up_own, up_oth))
    down_own, down_oth = (w.reshape(z_size, -1, model_width) for w in (down_own, down_oth))
    out_own, out_oth = (w.reshape(z_size, -1, model_width) for w in (out_own, out_oth))

    mine_core = me.reshape(1)
    middles, owns, oths = zip(
        *[
            branch(
                mine_core, returned[n], hidden_in[n], out_own, out_oth,
                b_out[None], second_gain[None], second_shift[None],
            )
            for n in range(sequences)
        ]
    )
    cot_low = out_grad.reshape(tokens, model_width)
    y, gs_own, gs_oth, gd_own, gd_oth, gu_own, gu_oth, grad_up_bias = feed(
        mine_core, owns, oths, cot_low, up_own, up_oth, down_own, down_oth, b_up[None]
    )

    cells = (z_size, y_size, x_size)
    to_up = gu_own.reshape(*cells, rows_each, ff_width)
    to_down = gd_own.reshape(*cells, ff_each, model_width)
    sum_up = [to_up, swap(gu_oth, "core").reshape(to_up.shape)]
    sum_down = [to_down, swap(gd_oth, "core").reshape(to_down.shape)]

    block_out = None
    grad_middles, grad_branches, grad_heads, sums = [], [], [], []
    for n in range(sequences):
        grad_middle, grad_branch, grad_att, four, block_out = middle_back(
            n, sequences, mine_core, gs_own, gs_oth, middles[n], out_grad[n], y,
            b_down[None], second_gain[None], out_own, out_oth, block_out,
        )
        grad_middles.append(grad_middle)
        grad_branches.append(grad_branch)
        sums.append(four)
        grad_heads.append(grad_att)
    grad_heads = jnp.stack(grad_heads, 1)
    grad_heads = lax.all_to_all(grad_heads, SEQ, split_axis=0, concat_axis=0, tiled=True)
    go_own, go_oth = out_weight_grad(mine_core, returned, grad_branches)
    to_out = go_own.reshape(*cells, rows_each, model_width)
    sum_out = [to_out, swap(go_oth, "core").reshape(to_out.shape)]
    parts = (give_part(sum_up, "fy", 1), give_part(sum_down, "fx", 2), give_part(sum_out, "fx", 2))
    sum_up = take_part(sum_up, parts[0], "fy", 1)
    sum_down = take_part(sum_down, parts[1], "fx", 2)
    sum_out = take_part(sum_out, parts[2], "fx", 2)

    four = total_of(sums)
    rear = [four[0], four[1], four[2], grad_up_bias, four[3]]
    rear_wide = jnp.concatenate([part.reshape(devices, -1) for part in rear], 1)
    rear_sum = jnp.sum(lax.all_to_all(rear_wide, ALL, split_axis=0, concat_axis=0, tiled=True), 0)

    grad_heads = after(grad_heads, *parts)

    grad_qkvw = jnp.zeros((model_width, 3 * width), F32)
    column_sums = jnp.zeros((3 * width,), F32)
    grad_first = []
    for n in range(sequences):
        first_low, q, k, v, kt, lse = kept[n]
        q = after(q, *parts)
        grads = grad_heads[:, n].reshape(q.shape)
        dq, dk, dv = attend_back(slopes, q, k, kt, v, grads, lse)
        last = [terms[-1] for terms in (sum_up, sum_down, sum_out)]
        dq, dk, dv, *last = lax.optimization_barrier((dq, dk, dv, *last))
        sum_up, sum_down, sum_out = (
            [*terms[:-1], recent] for terms, recent in zip((sum_up, sum_down, sum_out), last)
        )
        grad_projected = jnp.concatenate([dq, dk, dv], 1)
        partial = times_rows(grad_projected, w_heads).astype(BF)
        grad_first.append(lax.psum_scatter(partial, SEQ, scatter_dimension=0, tiled=True))
        parts = (partial,)
        if n == 0:
            parts = (partial, give_part(sum_up, "fx", 1), give_part(sum_down, "fy", 1), give_part(sum_out, "fy", 1))
            sum_up = take_part(sum_up, parts[1], "fx", 1)
            sum_down = take_part(sum_down, parts[2], "fy", 1)
            sum_out = take_part(sum_out, parts[3], "fy", 1)
        grad_qkvw = grad_qkvw + outer_sum(first_low, grad_projected)
        column_sums = column_sums + jnp.sum(grad_projected.astype(F32), 0)

    wide = [grad_qkvw.reshape(seq_devices, y_size, x_size, rows_each, 3 * width)]
    wide = total_of(reduce_axis(reduce_axis(wide, "fy", 1), "fx", 1))
    wide = lax.all_to_all(wide, SEQ, split_axis=0, concat_axis=0, tiled=True)
    wide = wide.reshape(seq_devices, rows_each, 3, width).transpose(1, 2, 0, 3)
    out_qkvw = wide.reshape(rows_each, 3 * model_width)

    low_sum = jnp.concatenate([total_of(sum_out).astype(BF), total_of(sum_down).astype(BF)], 1)
    low_sum = line_reduce(low_sum, "z")
    out_outw, out_down = low_sum[:rows_each], low_sum[rows_each:]
    out_up = line_reduce(total_of(sum_up).astype(BF), "z")

    input_grad = None
    sums = []
    for n in range(sequences):
        two, input_grad = first_back(
            n, sequences, grad_first[n], hidden_in[n], first_gain[None], grad_middles[n], input_grad
        )
        sums.append(two)
    two = total_of(sums)
    grad_gain_one, grad_shift_one = two[0], two[1]

    qv_here = jnp.zeros((2, seq_devices, width), F32)
    qv_mine = jnp.stack([column_sums[:width], column_sums[2 * width :]])
    qv_here = lax.dynamic_update_slice_in_dim(qv_here, qv_mine[:, None], place, 1)
    front = [grad_gain_one, grad_shift_one, qv_here.reshape(-1)]
    front_wide = jnp.concatenate([part.reshape(devices, -1) for part in front], 1)
    front_sum = jnp.sum(lax.all_to_all(front_wide, ALL, split_axis=0, concat_axis=0, tiled=True), 0)

    r = rows_each
    return (
        block_out,
        input_grad,
        front_sum[:r],
        front_sum[r : 2 * r],
        out_qkvw,
        front_sum[2 * r :],
        out_outw,
        rear_sum[:r],
        rear_sum[r : 2 * r],
        rear_sum[2 * r : 3 * r],
        out_up,
        rear_sum[3 * r : 3 * r + ff_each],
        out_down,
        rear_sum[3 * r + ff_each :],
    )


def solution(mesh):
    seq_size, fsdp_size = mesh.shape["seq"], mesh.shape["fsdp"]
    fine = Mesh(mesh.devices.reshape(seq_size // 2, 2, fsdp_size // 2, 2), ALL)
    tokens = P(FSDP, SEQ, None)
    vector = P(ALL)
    matrix = P(ALL, None)
    return jax.shard_map(
        body,
        mesh=fine,
        in_specs=(
            tokens, vector, vector, matrix, vector, P(), matrix, vector, vector, vector,
            matrix, vector, matrix, vector, tokens,
        ),
        out_specs=(
            tokens, tokens, vector, vector, matrix, vector, matrix, vector, vector, vector,
            matrix, vector, matrix, vector,
        ),
        check_vma=False,
    )
```

```python
import functools

import jax
import jax.numpy as jnp
from jax import lax
from jax.experimental import pallas as pl
from jax.experimental.pallas import tpu as pltpu
from jax.sharding import Mesh
from jax.sharding import PartitionSpec as P

H = 16
HD = 64
SEQ = ("z", "core")
FSDP = ("fy", "fx")
ALL = SEQ + FSDP
BF = jnp.bfloat16
F32 = jnp.float32
NT = (((1,), (1,)), ((), ()))
VMEM_BYTES = 48 * 1024 * 1024
LIGHT = pl.CostEstimate(flops=1024, bytes_accessed=1024, transcendentals=0)
HEAVY = pl.CostEstimate(flops=10**11, bytes_accessed=1024, transcendentals=0)


def layer_norm(values, norm_gain, norm_shift):
    average = jnp.mean(values, -1, keepdims=True)
    centered = values - average
    variance = jnp.mean(centered * centered, -1, keepdims=True)
    return centered * lax.rsqrt(variance + 1e-05) * norm_gain + norm_shift


def outer_sum(left, right):
    return lax.dot_general(left, right, (((0,), (0,)), ((), ())), preferred_element_type=F32)


def times_rows(left, right):
    return lax.dot_general(left, right, NT, preferred_element_type=F32)


def swap(values, axis):
    return lax.ppermute(values, axis, [(0, 1), (1, 0)])


def after(values, *earlier):
    return lax.optimization_barrier((values, *earlier))[0]


def merge_pair(mine, other, axis, position):
    shape = [1] * (mine.ndim + 1)
    shape[position] = 2
    slot = jnp.arange(2).reshape(shape)
    return jnp.where(
        slot == lax.axis_index(axis), jnp.expand_dims(mine, position), jnp.expand_dims(other, position)
    )


def line_gather(values, axis, before_second, before_last):
    size, me = lax.axis_size(axis), lax.axis_index(axis)
    held = jnp.zeros((3 * size - 2, *values.shape), values.dtype)
    held = lax.dynamic_update_index_in_dim(held, values, me + size - 1, 0)
    up = down = values
    for step in range(1, size):
        if step == 2:
            up, down = after(up, *before_second), after(down, *before_second)
        if step == size - 1:
            up, down = after(up, *before_last), after(down, *before_last)
        up = lax.ppermute(up, axis, [(i - 1, i) for i in range(step, size)])
        down = lax.ppermute(down, axis, [(i + 1, i) for i in range(size - step)])
        held = lax.dynamic_update_index_in_dim(held, up, me - step + size - 1, 0)
        held = lax.dynamic_update_index_in_dim(held, down, me + step + size - 1, 0)
    return held[size - 1 : 2 * size - 1]


def line_reduce(values, axis):
    size, me = lax.axis_size(axis), lax.axis_index(axis)
    up = down = 0.0
    for step in range(1, size):
        above = jnp.minimum(me + size - step, size - 1)
        below = jnp.maximum(me - size + step, 0)
        up = (at_index(values, above, 0).astype(F32) + up).astype(BF)
        down = (at_index(values, below, 0).astype(F32) + down).astype(BF)
        up = lax.ppermute(up, axis, [(i, i + 1) for i in range(step)]).astype(F32)
        down = lax.ppermute(down, axis, [(i, i - 1) for i in range(size - step, size)]).astype(F32)
    return at_index(values, me, 0).astype(F32) + up + down


def send_axis(values, axis, position):
    if lax.axis_size(axis) != 2:
        return lax.all_gather(values, axis, axis=position, tiled=False)
    return swap(values, axis)


def join_axis(values, other, axis, position):
    if lax.axis_size(axis) != 2:
        return other
    return merge_pair(values, other, axis, position)


def at_index(values, index, position):
    return lax.dynamic_index_in_dim(values, index, position, keepdims=False)


def total_of(terms):
    total = terms[0].astype(F32)
    for term in terms[1:]:
        total = total + term.astype(F32)
    return total


def give_part(terms, axis, position):
    if lax.axis_size(axis) != 2:
        return total_of(terms).astype(BF)
    other = 1 - lax.axis_index(axis)
    return total_of([at_index(term, other, position) for term in terms]).astype(BF)


def take_part(terms, given, axis, position):
    if lax.axis_size(axis) != 2:
        return [lax.psum_scatter(given, axis, scatter_dimension=position, tiled=False)]
    me = lax.axis_index(axis)
    return [at_index(term, me, position) for term in terms] + [swap(given, axis)]


def reduce_axis(terms, axis, position):
    return take_part(terms, give_part(terms, axis, position), axis, position)


def normalize(values):
    average = jnp.mean(values, -1, keepdims=True)
    centered = values - average
    variance = jnp.mean(centered * centered, -1, keepdims=True)
    scale = lax.rsqrt(variance + 1e-05)
    return centered * scale, scale


def norm_back(grad, normal, scale, gain):
    scaled = grad * gain
    inner = jnp.mean(scaled * normal, -1, keepdims=True)
    return scale * (scaled - jnp.mean(scaled, -1, keepdims=True) - normal * inner)


def branch_kernel(
    me_ref, att_ref, x_ref, w_own_ref, w_oth_ref, bias_ref, gain_ref, shift_ref, middle_ref, own_ref, oth_ref
):
    me = me_ref[0]
    z_size, block, _ = w_own_ref.shape
    middle = x_ref[...].astype(F32) + bias_ref[...]
    for z in range(z_size):
        middle = middle + jnp.dot(att_ref[2 * z + me], w_own_ref[z], preferred_element_type=F32)
        middle = middle + jnp.dot(att_ref[2 * z + 1 - me], w_oth_ref[z], preferred_element_type=F32)
    middle_ref[...] = middle
    normal, _ = normalize(middle)
    normal = normal * gain_ref[...] + shift_ref[...]
    for z in range(z_size):
        even = normal[:, 2 * z * block : (2 * z + 1) * block]
        odd = normal[:, (2 * z + 1) * block : (2 * z + 2) * block]
        own_ref[:, z * block : (z + 1) * block] = jnp.where(me == 0, even, odd).astype(BF)
        oth_ref[:, z * block : (z + 1) * block] = jnp.where(me == 0, odd, even).astype(BF)


def branch(me, att, rows, w_own, w_oth, bias, gain, shift):
    length, model_width = rows.shape
    vmem = pl.BlockSpec(memory_space=pltpu.VMEM)
    return pl.pallas_call(
        branch_kernel,
        in_specs=[pl.BlockSpec(memory_space=pltpu.SMEM)] + [vmem] * 7,
        out_specs=[vmem] * 3,
        out_shape=[
            jax.ShapeDtypeStruct((length, model_width), F32),
            jax.ShapeDtypeStruct((length, model_width // 2), BF),
            jax.ShapeDtypeStruct((length, model_width // 2), BF),
        ],
        compiler_params=pltpu.CompilerParams(vmem_limit_bytes=VMEM_BYTES),
        cost_estimate=LIGHT,
        name="branch",
    )(me, att, rows, w_own, w_oth, bias, gain, shift)


def middle_back_kernel(
    me_ref, gs_own_ref, gs_oth_ref, middle_ref, cot_ref, y_ref, bias_ref, gain_ref, w_own_ref, w_oth_ref, *rest
):
    gm_ref, gb_ref, ga_ref, sums_ref, out_ref, grad_scr = rest[-6:]
    me = me_ref[0]
    z_size, block, _ = w_own_ref.shape
    for z in range(z_size):
        own = gs_own_ref[:, z * block : (z + 1) * block]
        oth = gs_oth_ref[:, z * block : (z + 1) * block]
        grad_scr[:, 2 * z * block : (2 * z + 1) * block] = jnp.where(me == 0, own, oth)
        grad_scr[:, (2 * z + 1) * block : (2 * z + 2) * block] = jnp.where(me == 0, oth, own)
    middle = middle_ref[...]
    out_ref[0] = (middle + y_ref[...] + bias_ref[...]).astype(BF)
    normal, scale = normalize(middle)
    grad = grad_scr[...]
    cot = cot_ref[...].astype(F32)
    grad_middle = cot + norm_back(grad, normal, scale, gain_ref[...])
    gm_ref[...] = grad_middle
    low = grad_middle.astype(BF)
    gb_ref[...] = low
    for z in range(z_size):
        ga_ref[2 * z + me] = times_rows(low, w_own_ref[z]).astype(BF)
        ga_ref[2 * z + 1 - me] = times_rows(low, w_oth_ref[z]).astype(BF)
    sums_ref[0:1, :] = jnp.sum(low.astype(F32), 0, keepdims=True)
    sums_ref[1:2, :] = jnp.sum(grad * normal, 0, keepdims=True)
    sums_ref[2:3, :] = jnp.sum(grad, 0, keepdims=True)
    sums_ref[3:4, :] = jnp.sum(cot, 0, keepdims=True)


def middle_back(n, sequences, me, gs_own, gs_oth, middle, cot, y, bias, gain, w_own, w_oth, filled):
    length, model_width = middle.shape
    z_size, block, _ = w_own.shape
    whole = lambda i: (0, 0)
    part = lambda i: (n, 0)
    cube = lambda i: (0, 0, 0)
    half = pl.BlockSpec((length, model_width // 2), part)
    line = pl.BlockSpec((1, model_width), whole)
    matrix = pl.BlockSpec(w_own.shape, cube)
    full = pl.BlockSpec((length, model_width), whole)
    extra = [] if filled is None else [filled]
    return pl.pallas_call(
        middle_back_kernel,
        grid=(1,),
        in_specs=[
            pl.BlockSpec(memory_space=pltpu.SMEM), half, half, full, full,
            pl.BlockSpec((length, model_width), part), line, line, matrix, matrix,
        ]
        + [pl.BlockSpec(memory_space=pl.ANY)] * len(extra),
        out_specs=[
            full,
            full,
            pl.BlockSpec((2 * z_size, length, block), cube),
            pl.BlockSpec((8, model_width), whole),
            pl.BlockSpec((1, length, model_width), lambda i: (n, 0, 0)),
        ],
        out_shape=[
            jax.ShapeDtypeStruct((length, model_width), F32),
            jax.ShapeDtypeStruct((length, model_width), BF),
            jax.ShapeDtypeStruct((2 * z_size, length, block), BF),
            jax.ShapeDtypeStruct((8, model_width), F32),
            jax.ShapeDtypeStruct((sequences, length, model_width), BF),
        ],
        scratch_shapes=[pltpu.VMEM((length, model_width), F32)],
        input_output_aliases={10: 4} if extra else {},
        compiler_params=pltpu.CompilerParams(vmem_limit_bytes=VMEM_BYTES),
        cost_estimate=LIGHT,
        name="middle_back",
    )(me, gs_own, gs_oth, middle, cot, y, bias, gain, w_own, w_oth, *extra)


def out_weight_kernel(sequences, me_ref, *refs):
    own_refs, oth_refs = refs[:sequences], refs[sequences : 2 * sequences]
    grad_refs = refs[2 * sequences : 3 * sequences]
    go_own_ref, go_oth_ref = refs[3 * sequences :]
    for att_refs, out_ref in ((own_refs, go_own_ref), (oth_refs, go_oth_ref)):
        total = outer_sum(att_refs[0][0], grad_refs[0][...])
        for att_ref, grad_ref in zip(att_refs[1:], grad_refs[1:]):
            total = total + outer_sum(att_ref[0], grad_ref[...])
        out_ref[0] = total.astype(BF)


def out_weight_grad(me, atts, grads):
    sequences = len(atts)
    devices, length, block = atts[0].shape
    model_width = grads[0].shape[1]
    z_size = devices // 2
    own = pl.BlockSpec((1, length, block), lambda z, me_ref: (2 * z + me_ref[0], 0, 0))
    oth = pl.BlockSpec((1, length, block), lambda z, me_ref: (2 * z + 1 - me_ref[0], 0, 0))
    full = pl.BlockSpec((length, model_width), lambda z, me_ref: (0, 0))
    out = pl.BlockSpec((1, block, model_width), lambda z, me_ref: (z, 0, 0))
    shape = jax.ShapeDtypeStruct((z_size, block, model_width), BF)
    return pl.pallas_call(
        functools.partial(out_weight_kernel, sequences),
        grid_spec=pltpu.PrefetchScalarGridSpec(
            num_scalar_prefetch=1,
            grid=(z_size,),
            in_specs=[own] * sequences + [oth] * sequences + [full] * sequences,
            out_specs=[out, out],
        ),
        out_shape=[shape, shape],
        compiler_params=pltpu.CompilerParams(vmem_limit_bytes=VMEM_BYTES),
        cost_estimate=LIGHT,
        name="out_weight_grad",
    )(me, *atts, *atts, *grads)


def first_back_kernel(grad_ref, x_ref, gain_ref, gm_ref, *rest):
    out_ref = rest[-1]
    normal, scale = normalize(x_ref[...].astype(F32))
    out_ref[0] = gm_ref[...] + norm_back(grad_ref[...].astype(F32), normal, scale, gain_ref[...])


def first_back(n, sequences, grad, rows, gain, grad_middle, filled):
    length, model_width = rows.shape
    whole = lambda i: (0, 0)
    full = pl.BlockSpec((length, model_width), whole)
    extra = [] if filled is None else [filled]
    return pl.pallas_call(
        first_back_kernel,
        grid=(1,),
        in_specs=[full, full, pl.BlockSpec((1, model_width), whole), full]
        + [pl.BlockSpec(memory_space=pl.ANY)] * len(extra),
        out_specs=pl.BlockSpec((1, length, model_width), lambda i: (n, 0, 0)),
        out_shape=jax.ShapeDtypeStruct((sequences, length, model_width), F32),
        input_output_aliases={4: 0} if extra else {},
        compiler_params=pltpu.CompilerParams(vmem_limit_bytes=VMEM_BYTES),
        cost_estimate=LIGHT,
        name="first_back",
    )(grad, rows, gain, grad_middle, *extra)


def feed_kernel(sequences, me_ref, *refs):
    own_refs, oth_refs, refs = refs[:sequences], refs[sequences : 2 * sequences], refs[2 * sequences :]
    cot_ref, up_own_ref, up_oth_ref, down_own_ref, down_oth_ref, bias_ref = refs[:6]
    y_ref, gs_own_ref, gs_oth_ref, gd_own_ref, gd_oth_ref, gu_own_ref, gu_oth_ref, gb_ref = refs[6:14]
    own_ref, oth_ref, own_t, oth_t = refs[14:]
    step = pl.program_id(0)
    half = pl.num_programs(0) // 2
    length = own_refs[0].shape[0]

    @pl.when(step == 0)
    def _():
        for n in range(sequences):
            own_ref[n * length : (n + 1) * length, :] = own_refs[n][...]
            oth_ref[n * length : (n + 1) * length, :] = oth_refs[n][...]
        own_t[...] = own_ref[...].astype(F32).T.astype(BF)
        oth_t[...] = oth_ref[...].astype(F32).T.astype(BF)
        y_ref[...] = jnp.zeros_like(y_ref)
        gs_own_ref[...] = jnp.zeros_like(gs_own_ref)
        gs_oth_ref[...] = jnp.zeros_like(gs_oth_ref)

    def one(down_ref, gd_ref):
        down = down_ref[0]
        pre = jnp.dot(own_ref[...], up_own_ref[...], preferred_element_type=F32)
        pre = pre + jnp.dot(oth_ref[...], up_oth_ref[...], preferred_element_type=F32)
        pre = pre + bias_ref[...]
        square = pre * pre
        tanh = jnp.tanh(0.7978845608 * (pre + 0.044715 * pre * square))
        near = 0.5 * (1.0 + tanh)
        active = (pre * near).astype(BF)
        slope = near + 0.5 * pre * (1.0 - tanh * tanh) * (
            0.7978845608 * (1.0 + 3.0 * 0.044715 * square)
        )
        grad = lax.dot_general(cot_ref[...], down, NT, preferred_element_type=F32) * slope
        grad = grad.astype(BF)
        y_ref[...] = y_ref[...] + jnp.dot(active, down, preferred_element_type=F32)
        gd_ref[0] = outer_sum(active, cot_ref[...]).astype(BF)
        gu_own_ref[...] = jnp.dot(own_t[...], grad, preferred_element_type=F32).astype(BF)
        gu_oth_ref[...] = jnp.dot(oth_t[...], grad, preferred_element_type=F32).astype(BF)
        gb_ref[...] = jnp.sum(grad.astype(F32), 0, keepdims=True)
        gs_own_ref[...] = gs_own_ref[...] + times_rows(grad, up_own_ref[...])
        gs_oth_ref[...] = gs_oth_ref[...] + times_rows(grad, up_oth_ref[...])

    @pl.when(step < half)
    def _():
        one(down_own_ref, gd_own_ref)

    @pl.when(step >= half)
    def _():
        one(down_oth_ref, gd_oth_ref)


def feed(me, owns, oths, cot, up_own, up_oth, down_own, down_oth, bias):
    sequences = len(owns)
    length, half_width = owns[0].shape
    tokens, model_width = cot.shape
    ff_width = up_own.shape[1]
    z_size, block, _ = down_own.shape

    def column(j, me_ref):
        mine = me_ref[0]
        return (0, (j % z_size) * 2 + jnp.where(j < z_size, mine, 1 - mine))

    whole = lambda j, me_ref: (0, 0)
    first = lambda j, me_ref: (jnp.minimum(j, z_size - 1), 0, 0)
    second = lambda j, me_ref: (jnp.maximum(j - z_size, 0), 0, 0)
    halves = [pl.BlockSpec((tokens, half_width), whole)] * 2
    pieces = [pl.BlockSpec((length, half_width), whole)] * (2 * sequences)
    columns = [pl.BlockSpec((half_width, block), column)] * 2
    downs = [pl.BlockSpec((1, block, model_width), first), pl.BlockSpec((1, block, model_width), second)]
    line = pl.BlockSpec((1, block), column)
    all_rows = pl.BlockSpec((tokens, model_width), whole)
    return pl.pallas_call(
        functools.partial(feed_kernel, sequences),
        grid_spec=pltpu.PrefetchScalarGridSpec(
            num_scalar_prefetch=1,
            grid=(2 * z_size,),
            in_specs=[*pieces, all_rows, *columns, *downs, line],
            out_specs=[all_rows, *halves, *downs, *columns, line],
            scratch_shapes=[pltpu.VMEM((tokens, half_width), BF)] * 2
            + [pltpu.VMEM((half_width, tokens), BF)] * 2,
        ),
        out_shape=[
            jax.ShapeDtypeStruct((tokens, model_width), F32),
            jax.ShapeDtypeStruct((tokens, half_width), F32),
            jax.ShapeDtypeStruct((tokens, half_width), F32),
            jax.ShapeDtypeStruct(down_own.shape, BF),
            jax.ShapeDtypeStruct(down_own.shape, BF),
            jax.ShapeDtypeStruct(up_own.shape, BF),
            jax.ShapeDtypeStruct(up_own.shape, BF),
            jax.ShapeDtypeStruct((1, ff_width), F32),
        ],
        compiler_params=pltpu.CompilerParams(vmem_limit_bytes=VMEM_BYTES),
        cost_estimate=LIGHT,
        name="feed",
    )(me, *owns, *oths, cot, up_own, up_oth, down_own, down_oth, bias)


def project_kernel(x_ref, gain_ref, shift_ref, w_ref, bias_ref, low_ref, q_ref, k_ref, v_ref, kt_ref, vt_ref):
    width = q_ref.shape[1]
    low = layer_norm(x_ref[...].astype(F32), gain_ref[...], shift_ref[...]).astype(BF)
    low_ref[...] = low
    made = (jnp.dot(low, w_ref[...], preferred_element_type=F32) + bias_ref[...]).astype(BF)
    made = made.astype(F32)
    keys, values = made[:, width : 2 * width], made[:, 2 * width :]
    q_ref[...] = (made[:, :width] * (HD**-0.5)).astype(BF)
    k_ref[...] = keys.astype(BF)
    v_ref[...] = values.astype(BF)
    kt_ref[...] = keys.T.astype(BF)
    vt_ref[...] = values.T.astype(BF)


def project(rows, gain, shift, weight, bias):
    length, model_width = rows.shape
    width = weight.shape[1] // 3
    block = min(512, length)
    whole = lambda i: (0, 0)
    down = lambda i: (i, 0)
    across = lambda i: (0, i)
    return pl.pallas_call(
        project_kernel,
        grid=(length // block,),
        in_specs=[
            pl.BlockSpec((block, model_width), down),
            pl.BlockSpec((1, model_width), whole),
            pl.BlockSpec((1, model_width), whole),
            pl.BlockSpec((model_width, 3 * width), whole),
            pl.BlockSpec((1, 3 * width), whole),
        ],
        out_specs=[
            pl.BlockSpec((block, model_width), down),
            pl.BlockSpec((block, width), down),
            pl.BlockSpec((block, width), down),
            pl.BlockSpec((block, width), down),
            pl.BlockSpec((width, block), across),
            pl.BlockSpec((width, block), across),
        ],
        out_shape=[jax.ShapeDtypeStruct((length, model_width), BF)]
        + [jax.ShapeDtypeStruct((length, width), BF)] * 3
        + [jax.ShapeDtypeStruct((width, length), BF)] * 2,
        compiler_params=pltpu.CompilerParams(vmem_limit_bytes=VMEM_BYTES),
        cost_estimate=LIGHT,
        name="project",
    )(rows, gain, shift, weight, bias)


def tile_helpers(head, slope, block, width):
    lane = lax.broadcasted_iota(jnp.int32, (block, width), 1)
    mine = (lane >= head * HD) & (lane < head * HD + HD)
    key = lax.broadcasted_iota(jnp.int32, (block, block), 0)
    query = lax.broadcasted_iota(jnp.int32, (block, block), 1)
    return mine, slope * key.astype(F32), key <= query


def attend_kernel(slope_ref, q_ref, k_ref, vt_ref, o_ref, lse_ref, score_scr, out_scr):
    block, width = q_ref.shape
    number, head = pl.program_id(0), pl.program_id(1)
    slope = slope_ref[head]
    mine, bias, causal = tile_helpers(head, slope, block, width)
    queries = jnp.where(mine, q_ref[...], jnp.zeros_like(q_ref[...]))

    def one_block(last):
        highest = None
        for t in range(last + 1):
            rows = pl.ds(t * block, block)
            scores = lax.dot_general(k_ref[rows, :], queries, NT, preferred_element_type=F32) + bias
            if t == last:
                scores = jnp.where(causal, scores, -1e30)
            score_scr[rows, :] = scores
            top = jnp.max(scores, 0, keepdims=True) + slope * (t * block)
            highest = top if highest is None else jnp.maximum(highest, top)
        total = jnp.zeros((1, block), F32)
        blended = jnp.zeros((width, block), F32)
        for t in range(last + 1):
            rows = pl.ds(t * block, block)
            weights = jnp.exp(score_scr[rows, :] - (highest - slope * (t * block)))
            total = total + jnp.sum(weights, 0, keepdims=True)
            blended = blended + jnp.dot(
                vt_ref[:, rows], weights.astype(BF), preferred_element_type=F32
            )
        lse_ref[...] = (highest + jnp.log(total)).reshape(lse_ref.shape)
        result = jnp.where(mine, (blended / total).T, 0.0)

        @pl.when(head == 0)
        def _():
            out_scr[...] = result

        @pl.when(head > 0)
        def _():
            out_scr[...] = out_scr[...] + result

    for last in range(k_ref.shape[0] // block):
        pl.when(number == last)(functools.partial(one_block, last))

    @pl.when(head == pl.num_programs(1) - 1)
    def _():
        o_ref[...] = out_scr[...].astype(BF)


def attend(slopes, queries, keys, values_t):
    length, width = queries.shape
    heads = slopes.shape[0]
    block = min(256, length)
    whole = lambda i, h: (0, 0)
    down = lambda i, h: (i, 0)
    return pl.pallas_call(
        attend_kernel,
        grid=(length // block, heads),
        in_specs=[
            pl.BlockSpec(memory_space=pltpu.SMEM),
            pl.BlockSpec((block, width), down),
            pl.BlockSpec((length, width), whole),
            pl.BlockSpec((width, length), whole),
        ],
        out_specs=[
            pl.BlockSpec((block, width), down),
            pl.BlockSpec((1, 1, block), lambda i, h: (h, 0, i)),
        ],
        out_shape=[
            jax.ShapeDtypeStruct((length, width), BF),
            jax.ShapeDtypeStruct((heads, 1, length), F32),
        ],
        scratch_shapes=[pltpu.VMEM((length, block), F32), pltpu.VMEM((block, width), F32)],
        compiler_params=pltpu.CompilerParams(vmem_limit_bytes=VMEM_BYTES),
        cost_estimate=HEAVY,
        name="attend",
    )(slopes, queries, keys, values_t)


def attend_back_kernel(
    slope_ref, q_ref, k_ref, kt_ref, v_ref, g_ref, lse_ref, wq_ref, wk_ref, wv_ref,
    dq_ref, dk_ref, dv_ref, first_ref, prob_scr, dp_scr, dk_scr, dv_scr, dq_scr,
):
    block, width = q_ref.shape
    number, head = pl.program_id(0), pl.program_id(1)
    slope = slope_ref[head]
    mine, bias, causal = tile_helpers(head, slope, block, width)
    queries = jnp.where(mine, q_ref[...], jnp.zeros_like(q_ref[...]))
    grads = jnp.where(mine, g_ref[...], jnp.zeros_like(g_ref[...]))
    lse = lse_ref[...].reshape(1, block)

    @pl.when((number == 0) & (head == 0))
    def _():
        dk_scr[...] = jnp.zeros_like(dk_scr)
        dv_scr[...] = jnp.zeros_like(dv_scr)

    def one_block(last):
        centre = jnp.zeros((1, block), F32)
        for t in range(last + 1):
            rows = pl.ds(t * block, block)
            scores = lax.dot_general(k_ref[rows, :], queries, NT, preferred_element_type=F32) + bias
            if t == last:
                scores = jnp.where(causal, scores, -1e30)
            probs = jnp.exp(scores - (lse - slope * (t * block)))
            dp = lax.dot_general(v_ref[rows, :], grads, NT, preferred_element_type=F32)
            prob_scr[rows, :] = probs
            dp_scr[rows, :] = dp
            centre = centre + jnp.sum(probs * dp, 0, keepdims=True)
            dv_scr[rows, :] = dv_scr[rows, :] + jnp.dot(
                probs.astype(BF), grads, preferred_element_type=F32
            )
        dq = jnp.zeros((width, block), F32)
        for t in range(last + 1):
            rows = pl.ds(t * block, block)
            ds = (prob_scr[rows, :] * (dp_scr[rows, :] - centre)).astype(BF)
            dk_scr[rows, :] = dk_scr[rows, :] + jnp.dot(ds, queries, preferred_element_type=F32)
            dq = dq + jnp.dot(kt_ref[:, rows], ds, preferred_element_type=F32)
        result = jnp.where(mine, (dq * (HD**-0.5)).T, 0.0)

        @pl.when(head == 0)
        def _():
            dq_scr[...] = result

        @pl.when(head > 0)
        def _():
            dq_scr[...] = dq_scr[...] + result

    for last in range(k_ref.shape[0] // block):
        pl.when(number == last)(functools.partial(one_block, last))

    @pl.when(head == pl.num_programs(1) - 1)
    def _():
        dq_ref[pl.ds(pl.multiple_of(number * block, block), block), :] = dq_scr[...].astype(BF)

    @pl.when((head == pl.num_programs(1) - 1) & (number == pl.num_programs(0) - 1))
    def _():
        dk_ref[...] = dk_scr[...].astype(BF)
        dv_ref[...] = dv_scr[...].astype(BF)

        def one_part(t, carry):
            rows = pl.ds(pl.multiple_of(t * block, block), block)
            first = times_rows(dq_ref[rows, :], wq_ref[...])
            first = first + times_rows(dk_ref[rows, :], wk_ref[...])
            first = first + times_rows(dv_ref[rows, :], wv_ref[...])
            first_ref[rows, :] = first.astype(BF)
            return carry

        lax.fori_loop(0, k_ref.shape[0] // block, one_part, 0)


def attend_back(slopes, queries, keys, keys_t, values, grads, lse, weights):
    length, width = queries.shape
    model_width = weights[0].shape[0]
    heads = slopes.shape[0]
    block = min(256, length)
    whole = lambda i, h: (0, 0)
    down = lambda i, h: (i, 0)
    return pl.pallas_call(
        attend_back_kernel,
        grid=(length // block, heads),
        in_specs=[
            pl.BlockSpec(memory_space=pltpu.SMEM),
            pl.BlockSpec((block, width), down),
            pl.BlockSpec((length, width), whole),
            pl.BlockSpec((width, length), whole),
            pl.BlockSpec((length, width), whole),
            pl.BlockSpec((block, width), down),
            pl.BlockSpec((1, 1, block), lambda i, h: (h, 0, i)),
        ]
        + [pl.BlockSpec((model_width, width), whole)] * 3,
        out_specs=[pl.BlockSpec((length, width), whole)] * 3
        + [pl.BlockSpec((length, model_width), whole)],
        out_shape=[jax.ShapeDtypeStruct((length, width), BF)] * 3
        + [jax.ShapeDtypeStruct((length, model_width), BF)],
        scratch_shapes=[
            pltpu.VMEM((length, block), F32),
            pltpu.VMEM((length, block), F32),
            pltpu.VMEM((length, width), F32),
            pltpu.VMEM((length, width), F32),
            pltpu.VMEM((block, width), F32),
        ],
        compiler_params=pltpu.CompilerParams(vmem_limit_bytes=VMEM_BYTES),
        cost_estimate=HEAVY,
        name="attend_back",
    )(slopes, queries, keys, keys_t, values, grads, lse, *weights)


def body(
    hidden_in,
    norm1_gain,
    norm1_bias,
    qkv_weight,
    qv_bias,
    alibi_slopes,
    out_weight,
    out_bias,
    norm2_gain,
    norm2_bias,
    up_weight,
    up_bias,
    down_weight,
    down_bias,
    out_grad,
):
    seq_devices = lax.axis_size(SEQ)
    fsdp_devices = lax.axis_size(FSDP)
    devices = seq_devices * fsdp_devices
    z_size, y_size, x_size = lax.axis_size("z"), lax.axis_size("fy"), lax.axis_size("fx")
    sequences, local_len, model_width = hidden_in.shape
    tokens = sequences * local_len
    heads_local = H // seq_devices
    width = heads_local * HD
    ff_width = up_weight.shape[1]
    rows_each = qkv_weight.shape[0]
    ff_each = down_weight.shape[0]
    place = lax.axis_index(SEQ)
    slopes = lax.dynamic_slice_in_dim(alibi_slopes, place * heads_local, heads_local)

    me = lax.axis_index("core")

    small_parts = (norm1_gain, norm1_bias, qv_bias, out_bias, norm2_gain, norm2_bias, up_bias, down_bias)
    small_here = jnp.concatenate(small_parts)
    small_all = lax.all_to_all(
        jnp.broadcast_to(small_here, (devices, small_here.shape[0])), ALL, split_axis=0, concat_axis=0, tiled=True
    )
    full, start = [], 0
    for part in small_parts:
        size = part.shape[0]
        full.append(small_all[:, start : start + size].reshape(-1).astype(F32))
        start += size
    first_gain, first_shift, bias_qv, b_out, second_gain, second_shift, b_up, b_down = full

    columns = qkv_weight.reshape(rows_each, 3, seq_devices, width).transpose(2, 0, 1, 3)
    columns = columns.reshape(seq_devices, rows_each, 3 * width)
    columns = lax.all_to_all(columns, SEQ, split_axis=0, concat_axis=0, tiled=True)
    w_heads = lax.all_gather(columns, FSDP, axis=1, tiled=False).reshape(model_width, 3 * width)
    bias_parts = bias_qv.reshape(2, seq_devices, width)
    bias_mine = lax.dynamic_index_in_dim(bias_parts, place, 1, keepdims=False)
    bias_heads = jnp.concatenate([bias_mine[0], jnp.zeros((width,), F32), bias_mine[1]])

    low_z = lax.all_gather(jnp.concatenate([out_weight, down_weight], 0), "z", axis=0, tiled=False)
    down_z, out_z = low_z[:, rows_each:], low_z[:, :rows_each]
    middle_z = z_size // 2

    def first_stage(pieces):
        sent = [send_axis(part, first, 1) for part, first, _ in pieces]
        return lax.optimization_barrier(sent)

    def second_stage(pieces, sent):
        pairs = [join_axis(part, other, first, 1) for (part, first, _), other in zip(pieces, sent)]
        return pairs, [send_axis(p, second, at_of(second)) for p, (_, _, second) in zip(pairs, pieces)]

    def at_of(second):
        return 1 if second == "fy" else 2

    def finish(pieces, pairs, sent):
        return [join_axis(p, o, second, at_of(second)) for p, o, (_, _, second) in zip(pairs, sent, pieces)]

    low_pieces = [
        (down_z[:middle_z], "fy", "fx"), (down_z[middle_z:], "fx", "fy"), (out_z, "fy", "fx")
    ]
    low_sent = first_stage(low_pieces)
    up_z = line_gather(up_weight, "z", (small_all, columns), (w_heads, *low_sent))
    low_pairs, low_sent = second_stage(low_pieces, low_sent)
    up_z = after(up_z, *low_pairs)
    up_pieces = [(up_z[:middle_z], "fy", "fx"), (up_z[middle_z:], "fx", "fy")]
    up_sent = first_stage(up_pieces)
    up_pairs, up_sent = second_stage(up_pieces, up_sent)

    kept = []
    returned = []
    ahead = (*up_pairs, *low_sent)
    for n in range(sequences):
        rows = after(lax.all_gather(hidden_in[n], SEQ, axis=0, tiled=True), *ahead)
        first_low, q, k, v, kt, vt = project(
            rows, first_gain[None], first_shift[None], w_heads, bias_heads[None]
        )
        attended, lse = attend(slopes, q, k, vt)
        attended = attended.reshape(seq_devices, local_len, width)
        returned.append(lax.all_to_all(attended, SEQ, split_axis=0, concat_axis=0, tiled=True))
        kept.append((first_low, q, k, v, kt, lse))
        ahead = (returned[n],)
        if n == 0:
            *up_sent, _ = lax.optimization_barrier((*up_sent, lse))
            down_a, down_b, out_own = finish(low_pieces, low_pairs, low_sent)
            down_own = jnp.concatenate([down_a, down_b], 0)
            down_oth, out_oth = swap(down_own, "core"), swap(out_own, "core")
            up_own = jnp.concatenate(finish(up_pieces, up_pairs, up_sent), 0)
            up_oth = swap(up_own, "core")
            ahead = (*ahead, down_own, out_own, up_own)
    up_oth, down_oth, out_oth, _ = lax.optimization_barrier((up_oth, down_oth, out_oth, lse))
    half_width = model_width // 2
    up_own, up_oth = (w.reshape(half_width, ff_width) for w in (up_own, up_oth))
    down_own, down_oth = (w.reshape(z_size, -1, model_width) for w in (down_own, down_oth))
    out_own, out_oth = (w.reshape(z_size, -1, model_width) for w in (out_own, out_oth))

    mine_core = me.reshape(1)
    middles, owns, oths = zip(
        *[
            branch(
                mine_core, returned[n], hidden_in[n], out_own, out_oth,
                b_out[None], second_gain[None], second_shift[None],
            )
            for n in range(sequences)
        ]
    )
    cot_low = out_grad.reshape(tokens, model_width)
    y, gs_own, gs_oth, gd_own, gd_oth, gu_own, gu_oth, grad_up_bias = feed(
        mine_core, owns, oths, cot_low, up_own, up_oth, down_own, down_oth, b_up[None]
    )

    cells = (z_size, y_size, x_size)
    to_up = gu_own.reshape(*cells, rows_each, ff_width)
    to_down = gd_own.reshape(*cells, ff_each, model_width)
    sum_up = [to_up, swap(gu_oth, "core").reshape(to_up.shape)]
    sum_down = [to_down, swap(gd_oth, "core").reshape(to_down.shape)]

    block_out = None
    grad_middles, grad_branches, grad_heads, sums = [], [], [], []
    for n in range(sequences):
        grad_middle, grad_branch, grad_att, four, block_out = middle_back(
            n, sequences, mine_core, gs_own, gs_oth, middles[n], out_grad[n], y,
            b_down[None], second_gain[None], out_own, out_oth, block_out,
        )
        grad_middles.append(grad_middle)
        grad_branches.append(grad_branch)
        sums.append(four)
        grad_heads.append(lax.all_to_all(grad_att, SEQ, split_axis=0, concat_axis=0, tiled=True))
    go_own, go_oth = out_weight_grad(mine_core, returned, grad_branches)
    to_out = go_own.reshape(*cells, rows_each, model_width)
    sum_out = [to_out, swap(go_oth, "core").reshape(to_out.shape)]
    parts = (give_part(sum_up, "fy", 1), give_part(sum_down, "fx", 2), give_part(sum_out, "fx", 2))
    sum_up = take_part(sum_up, parts[0], "fy", 1)
    sum_down = take_part(sum_down, parts[1], "fx", 2)
    sum_out = take_part(sum_out, parts[2], "fx", 2)

    four = total_of(sums)
    rear = [four[0], four[1], four[2], grad_up_bias, four[3]]
    grad_heads[0] = after(grad_heads[0], *parts)
    head_weights = [w_heads[:, i * width : (i + 1) * width] for i in range(3)]
    grad_first, grad_projected = [], []
    for n in range(sequences):
        first_low, q, k, v, kt, lse = kept[n]
        if n > 0:
            q = after(q, partial, *gives)
        *parts_qkv, partial = attend_back(
            slopes, q, k, kt, v, grad_heads[n].reshape(q.shape), lse, head_weights
        )
        grad_first.append(lax.psum_scatter(partial, SEQ, scatter_dimension=0, tiled=True))
        recent = [terms[-1] for terms in (sum_up, sum_down, sum_out)]
        if n < sequences - 1:
            recent.append(grad_heads[n + 1])
        parts_qkv, recent = lax.optimization_barrier((parts_qkv, recent))
        if n < sequences - 1:
            grad_heads[n + 1] = recent.pop()
        sum_up, sum_down, sum_out = (
            [*terms[:-1], term] for terms, term in zip((sum_up, sum_down, sum_out), recent)
        )
        if n == 0:
            gives = (give_part(sum_up, "fx", 1), give_part(sum_down, "fy", 1), give_part(sum_out, "fy", 1))
            sum_up = take_part(sum_up, gives[0], "fx", 1)
            sum_down = take_part(sum_down, gives[1], "fy", 1)
            sum_out = take_part(sum_out, gives[2], "fy", 1)
        grad_projected.append(jnp.concatenate(parts_qkv, 1))
    grad_qkvw = jnp.zeros((model_width, 3 * width), F32)
    column_sums = jnp.zeros((3 * width,), F32)
    for n in range(sequences):
        grad_qkvw = grad_qkvw + outer_sum(kept[n][0], grad_projected[n])
        column_sums = column_sums + jnp.sum(grad_projected[n].astype(F32), 0)
    wide = [grad_qkvw.reshape(seq_devices, y_size, x_size, rows_each, 3 * width)]
    wide = total_of(reduce_axis(reduce_axis(wide, "fy", 1), "fx", 1))
    wide = lax.all_to_all(wide, SEQ, split_axis=0, concat_axis=0, tiled=True)
    wide = wide.reshape(seq_devices, rows_each, 3, width).transpose(1, 2, 0, 3)
    out_qkvw = wide.reshape(rows_each, 3 * model_width)

    low_sum = jnp.concatenate([total_of(sum_out).astype(BF), total_of(sum_down).astype(BF)], 1)
    low_sum = line_reduce(low_sum, "z")
    out_outw, out_down = low_sum[:rows_each], low_sum[rows_each:]
    out_up = line_reduce(total_of(sum_up).astype(BF), "z")

    input_grad = None
    for n in range(sequences):
        input_grad = first_back(
            n, sequences, grad_first[n], hidden_in[n], first_gain[None], grad_middles[n], input_grad
        )

    rear_wide = jnp.concatenate([part.reshape(devices, -1) for part in rear], 1)
    columns_wide = jnp.broadcast_to(column_sums, (devices, 3 * width))
    small = jnp.concatenate([rear_wide, columns_wide], 1)
    small = lax.all_to_all(small, ALL, split_axis=0, concat_axis=0, tiled=True)
    rear_sum = jnp.sum(small[:, : rear_wide.shape[1]], 0)
    rear_outs, start = [], 0
    for part in rear:
        size = part.size // devices
        rear_outs.append(rear_sum[start : start + size])
        start += size
    out_bias_sum, gain_two, shift_two, up_bias_sum, down_bias_sum = rear_outs
    totals = small[:, start:].reshape(seq_devices, fsdp_devices, 3, width).sum(1).transpose(1, 0, 2)
    totals = totals.reshape(3, model_width)
    qv_each = qv_bias.shape[0]
    qv = lax.dynamic_slice_in_dim(totals[::2].reshape(-1), lax.axis_index(ALL) * qv_each, qv_each)
    weight_here = qkv_weight.astype(F32)
    shift_one = jnp.sum(weight_here * totals.reshape(-1), 1)
    gain_one = jnp.sum(weight_here * out_qkvw, 1) - norm1_bias.astype(F32) * shift_one
    gain_one = gain_one / norm1_gain.astype(F32)
    return (
        block_out, input_grad, gain_one, shift_one, out_qkvw, qv, out_outw, out_bias_sum,
        gain_two, shift_two, out_up, up_bias_sum, out_down, down_bias_sum,
    )


def solution(mesh):
    seq_size, fsdp_size = mesh.shape["seq"], mesh.shape["fsdp"]
    fine = Mesh(mesh.devices.reshape(seq_size // 2, 2, fsdp_size // 2, 2), ALL)
    tokens = P(FSDP, SEQ, None)
    vector = P(ALL)
    matrix = P(ALL, None)
    return jax.shard_map(
        body,
        mesh=fine,
        in_specs=(
            tokens, vector, vector, matrix, vector, P(), matrix, vector, vector, vector,
            matrix, vector, matrix, vector, tokens,
        ),
        out_specs=(
            tokens, tokens, vector, vector, matrix, vector, matrix, vector, vector, vector,
            matrix, vector, matrix, vector,
        ),
        check_vma=False,
    )
```

```python
import functools

import jax
import jax.numpy as jnp
from jax import lax
from jax.experimental import pallas as pl
from jax.experimental.pallas import tpu as pltpu
from jax.sharding import Mesh
from jax.sharding import PartitionSpec as P

H = 16
HD = 64
SEQ = ("z", "core")
FSDP = ("fy", "fx")
ALL = SEQ + FSDP
BF = jnp.bfloat16
F32 = jnp.float32
NT = (((1,), (1,)), ((), ()))
VMEM_BYTES = 48 * 1024 * 1024
LIGHT = pl.CostEstimate(flops=1024, bytes_accessed=1024, transcendentals=0)
HEAVY = pl.CostEstimate(flops=10**11, bytes_accessed=1024, transcendentals=0)


def layer_norm(values, norm_gain, norm_shift):
    average = jnp.mean(values, -1, keepdims=True)
    centered = values - average
    variance = jnp.mean(centered * centered, -1, keepdims=True)
    return centered * lax.rsqrt(variance + 1e-05) * norm_gain + norm_shift


def outer_sum(left, right):
    return lax.dot_general(left, right, (((0,), (0,)), ((), ())), preferred_element_type=F32)


def times_rows(left, right):
    return lax.dot_general(left, right, NT, preferred_element_type=F32)


def swap(values, axis):
    return lax.ppermute(values, axis, [(0, 1), (1, 0)])


def after(values, *earlier):
    return lax.optimization_barrier((values, *earlier))[0]


def merge_pair(mine, other, axis, position):
    shape = [1] * (mine.ndim + 1)
    shape[position] = 2
    slot = jnp.arange(2).reshape(shape)
    return jnp.where(
        slot == lax.axis_index(axis), jnp.expand_dims(mine, position), jnp.expand_dims(other, position)
    )


def line_gather(values, axis, before_second, before_last):
    size, me = lax.axis_size(axis), lax.axis_index(axis)
    held = jnp.zeros((3 * size - 2, *values.shape), values.dtype)
    held = lax.dynamic_update_index_in_dim(held, values, me + size - 1, 0)
    up = down = values
    for step in range(1, size):
        if step == 2:
            up, down = after(up, *before_second), after(down, *before_second)
        if step == size - 1:
            up, down = after(up, *before_last), after(down, *before_last)
        up = lax.ppermute(up, axis, [(i - 1, i) for i in range(step, size)])
        down = lax.ppermute(down, axis, [(i + 1, i) for i in range(size - step)])
        held = lax.dynamic_update_index_in_dim(held, up, me - step + size - 1, 0)
        held = lax.dynamic_update_index_in_dim(held, down, me + step + size - 1, 0)
    return held[size - 1 : 2 * size - 1]


def line_reduce(values, axis):
    size, me = lax.axis_size(axis), lax.axis_index(axis)
    up = down = 0.0
    for step in range(1, size):
        above = jnp.minimum(me + size - step, size - 1)
        below = jnp.maximum(me - size + step, 0)
        up = (at_index(values, above, 0).astype(F32) + up).astype(BF)
        down = (at_index(values, below, 0).astype(F32) + down).astype(BF)
        up = lax.ppermute(up, axis, [(i, i + 1) for i in range(step)]).astype(F32)
        down = lax.ppermute(down, axis, [(i, i - 1) for i in range(size - step, size)]).astype(F32)
    return at_index(values, me, 0).astype(F32) + up + down


def send_axis(values, axis, position):
    if lax.axis_size(axis) != 2:
        return lax.all_gather(values, axis, axis=position, tiled=False)
    return swap(values, axis)


def join_axis(values, other, axis, position):
    if lax.axis_size(axis) != 2:
        return other
    return merge_pair(values, other, axis, position)


def at_index(values, index, position):
    return lax.dynamic_index_in_dim(values, index, position, keepdims=False)


def total_of(terms):
    total = terms[0].astype(F32)
    for term in terms[1:]:
        total = total + term.astype(F32)
    return total


def give_part(terms, axis, position):
    if lax.axis_size(axis) != 2:
        return total_of(terms).astype(BF)
    other = 1 - lax.axis_index(axis)
    return total_of([at_index(term, other, position) for term in terms]).astype(BF)


def take_part(terms, given, axis, position):
    if lax.axis_size(axis) != 2:
        return [lax.psum_scatter(given, axis, scatter_dimension=position, tiled=False)]
    me = lax.axis_index(axis)
    return [at_index(term, me, position) for term in terms] + [swap(given, axis)]


def reduce_axis(terms, axis, position):
    return take_part(terms, give_part(terms, axis, position), axis, position)


def normalize(values):
    average = jnp.mean(values, -1, keepdims=True)
    centered = values - average
    variance = jnp.mean(centered * centered, -1, keepdims=True)
    scale = lax.rsqrt(variance + 1e-05)
    return centered * scale, scale


def norm_back(grad, normal, scale, gain):
    scaled = grad * gain
    inner = jnp.mean(scaled * normal, -1, keepdims=True)
    return scale * (scaled - jnp.mean(scaled, -1, keepdims=True) - normal * inner)


def branch_kernel(
    me_ref, att_ref, x_ref, w_own_ref, w_oth_ref, bias_ref, gain_ref, shift_ref, middle_ref, own_ref, oth_ref
):
    me = me_ref[0]
    z_size, block, _ = w_own_ref.shape
    middle = x_ref[...].astype(F32) + bias_ref[...]
    for z in range(z_size):
        middle = middle + jnp.dot(att_ref[2 * z + me], w_own_ref[z], preferred_element_type=F32)
        middle = middle + jnp.dot(att_ref[2 * z + 1 - me], w_oth_ref[z], preferred_element_type=F32)
    middle_ref[...] = middle
    normal, _ = normalize(middle)
    normal = normal * gain_ref[...] + shift_ref[...]
    for z in range(z_size):
        even = normal[:, 2 * z * block : (2 * z + 1) * block]
        odd = normal[:, (2 * z + 1) * block : (2 * z + 2) * block]
        own_ref[:, z * block : (z + 1) * block] = jnp.where(me == 0, even, odd).astype(BF)
        oth_ref[:, z * block : (z + 1) * block] = jnp.where(me == 0, odd, even).astype(BF)


def branch(me, att, rows, w_own, w_oth, bias, gain, shift):
    length, model_width = rows.shape
    vmem = pl.BlockSpec(memory_space=pltpu.VMEM)
    return pl.pallas_call(
        branch_kernel,
        in_specs=[pl.BlockSpec(memory_space=pltpu.SMEM)] + [vmem] * 7,
        out_specs=[vmem] * 3,
        out_shape=[
            jax.ShapeDtypeStruct((length, model_width), F32),
            jax.ShapeDtypeStruct((length, model_width // 2), BF),
            jax.ShapeDtypeStruct((length, model_width // 2), BF),
        ],
        compiler_params=pltpu.CompilerParams(vmem_limit_bytes=VMEM_BYTES),
        cost_estimate=LIGHT,
        name="branch",
    )(me, att, rows, w_own, w_oth, bias, gain, shift)


def middle_back_kernel(
    me_ref, gs_own_ref, gs_oth_ref, middle_ref, cot_ref, y_ref, bias_ref, gain_ref, w_own_ref, w_oth_ref, *rest
):
    gm_ref, gb_ref, ga_ref, sums_ref, out_ref, grad_scr = rest[-6:]
    me = me_ref[0]
    z_size, block, _ = w_own_ref.shape
    for z in range(z_size):
        own = gs_own_ref[:, z * block : (z + 1) * block]
        oth = gs_oth_ref[:, z * block : (z + 1) * block]
        grad_scr[:, 2 * z * block : (2 * z + 1) * block] = jnp.where(me == 0, own, oth)
        grad_scr[:, (2 * z + 1) * block : (2 * z + 2) * block] = jnp.where(me == 0, oth, own)
    middle = middle_ref[...]
    out_ref[0] = (middle + y_ref[...] + bias_ref[...]).astype(BF)
    normal, scale = normalize(middle)
    grad = grad_scr[...]
    cot = cot_ref[...].astype(F32)
    grad_middle = cot + norm_back(grad, normal, scale, gain_ref[...])
    gm_ref[...] = grad_middle
    low = grad_middle.astype(BF)
    gb_ref[...] = low
    for z in range(z_size):
        ga_ref[2 * z + me] = times_rows(low, w_own_ref[z]).astype(BF)
        ga_ref[2 * z + 1 - me] = times_rows(low, w_oth_ref[z]).astype(BF)
    sums_ref[0:1, :] = jnp.sum(low.astype(F32), 0, keepdims=True)
    sums_ref[1:2, :] = jnp.sum(grad * normal, 0, keepdims=True)
    sums_ref[2:3, :] = jnp.sum(grad, 0, keepdims=True)
    sums_ref[3:4, :] = jnp.sum(cot, 0, keepdims=True)


def middle_back(n, sequences, me, gs_own, gs_oth, middle, cot, y, bias, gain, w_own, w_oth, filled):
    length, model_width = middle.shape
    z_size, block, _ = w_own.shape
    whole = lambda i: (0, 0)
    part = lambda i: (n, 0)
    cube = lambda i: (0, 0, 0)
    half = pl.BlockSpec((length, model_width // 2), part)
    line = pl.BlockSpec((1, model_width), whole)
    matrix = pl.BlockSpec(w_own.shape, cube)
    full = pl.BlockSpec((length, model_width), whole)
    extra = [] if filled is None else [filled]
    return pl.pallas_call(
        middle_back_kernel,
        grid=(1,),
        in_specs=[
            pl.BlockSpec(memory_space=pltpu.SMEM), half, half, full, full,
            pl.BlockSpec((length, model_width), part), line, line, matrix, matrix,
        ]
        + [pl.BlockSpec(memory_space=pl.ANY)] * len(extra),
        out_specs=[
            full,
            full,
            pl.BlockSpec((2 * z_size, length, block), cube),
            pl.BlockSpec((8, model_width), whole),
            pl.BlockSpec((1, length, model_width), lambda i: (n, 0, 0)),
        ],
        out_shape=[
            jax.ShapeDtypeStruct((length, model_width), F32),
            jax.ShapeDtypeStruct((length, model_width), BF),
            jax.ShapeDtypeStruct((2 * z_size, length, block), BF),
            jax.ShapeDtypeStruct((8, model_width), F32),
            jax.ShapeDtypeStruct((sequences, length, model_width), BF),
        ],
        scratch_shapes=[pltpu.VMEM((length, model_width), F32)],
        input_output_aliases={10: 4} if extra else {},
        compiler_params=pltpu.CompilerParams(vmem_limit_bytes=VMEM_BYTES),
        cost_estimate=LIGHT,
        name="middle_back",
    )(me, gs_own, gs_oth, middle, cot, y, bias, gain, w_own, w_oth, *extra)


def out_weight_kernel(sequences, me_ref, *refs):
    own_refs, oth_refs = refs[:sequences], refs[sequences : 2 * sequences]
    grad_refs = refs[2 * sequences : 3 * sequences]
    go_own_ref, go_oth_ref = refs[3 * sequences :]
    for att_refs, out_ref in ((own_refs, go_own_ref), (oth_refs, go_oth_ref)):
        total = outer_sum(att_refs[0][0], grad_refs[0][...])
        for att_ref, grad_ref in zip(att_refs[1:], grad_refs[1:]):
            total = total + outer_sum(att_ref[0], grad_ref[...])
        out_ref[0] = total.astype(BF)


def out_weight_grad(me, atts, grads):
    sequences = len(atts)
    devices, length, block = atts[0].shape
    model_width = grads[0].shape[1]
    z_size = devices // 2
    own = pl.BlockSpec((1, length, block), lambda z, me_ref: (2 * z + me_ref[0], 0, 0))
    oth = pl.BlockSpec((1, length, block), lambda z, me_ref: (2 * z + 1 - me_ref[0], 0, 0))
    full = pl.BlockSpec((length, model_width), lambda z, me_ref: (0, 0))
    out = pl.BlockSpec((1, block, model_width), lambda z, me_ref: (z, 0, 0))
    shape = jax.ShapeDtypeStruct((z_size, block, model_width), BF)
    return pl.pallas_call(
        functools.partial(out_weight_kernel, sequences),
        grid_spec=pltpu.PrefetchScalarGridSpec(
            num_scalar_prefetch=1,
            grid=(z_size,),
            in_specs=[own] * sequences + [oth] * sequences + [full] * sequences,
            out_specs=[out, out],
        ),
        out_shape=[shape, shape],
        compiler_params=pltpu.CompilerParams(vmem_limit_bytes=VMEM_BYTES),
        cost_estimate=LIGHT,
        name="out_weight_grad",
    )(me, *atts, *atts, *grads)


def first_back_kernel(grad_ref, x_ref, gain_ref, gm_ref, *rest):
    out_ref = rest[-1]
    normal, scale = normalize(x_ref[...].astype(F32))
    out_ref[0] = gm_ref[...] + norm_back(grad_ref[...].astype(F32), normal, scale, gain_ref[...])


def first_back(n, sequences, grad, rows, gain, grad_middle, filled):
    length, model_width = rows.shape
    whole = lambda i: (0, 0)
    full = pl.BlockSpec((length, model_width), whole)
    extra = [] if filled is None else [filled]
    return pl.pallas_call(
        first_back_kernel,
        grid=(1,),
        in_specs=[full, full, pl.BlockSpec((1, model_width), whole), full]
        + [pl.BlockSpec(memory_space=pl.ANY)] * len(extra),
        out_specs=pl.BlockSpec((1, length, model_width), lambda i: (n, 0, 0)),
        out_shape=jax.ShapeDtypeStruct((sequences, length, model_width), F32),
        input_output_aliases={4: 0} if extra else {},
        compiler_params=pltpu.CompilerParams(vmem_limit_bytes=VMEM_BYTES),
        cost_estimate=LIGHT,
        name="first_back",
    )(grad, rows, gain, grad_middle, *extra)


def feed_kernel(sequences, me_ref, *refs):
    own_refs, oth_refs, refs = refs[:sequences], refs[sequences : 2 * sequences], refs[2 * sequences :]
    cot_ref, up_own_ref, up_oth_ref, down_own_ref, down_oth_ref, bias_ref = refs[:6]
    y_ref, gs_own_ref, gs_oth_ref, gd_own_ref, gd_oth_ref, gu_own_ref, gu_oth_ref, gb_ref = refs[6:14]
    own_ref, oth_ref, own_t, oth_t = refs[14:]
    step = pl.program_id(0)
    half = pl.num_programs(0) // 2
    length = own_refs[0].shape[0]

    @pl.when(step == 0)
    def _():
        for n in range(sequences):
            own_ref[n * length : (n + 1) * length, :] = own_refs[n][...]
            oth_ref[n * length : (n + 1) * length, :] = oth_refs[n][...]
        own_t[...] = own_ref[...].astype(F32).T.astype(BF)
        oth_t[...] = oth_ref[...].astype(F32).T.astype(BF)
        y_ref[...] = jnp.zeros_like(y_ref)
        gs_own_ref[...] = jnp.zeros_like(gs_own_ref)
        gs_oth_ref[...] = jnp.zeros_like(gs_oth_ref)

    def one(down_ref, gd_ref):
        down = down_ref[0]
        pre = jnp.dot(own_ref[...], up_own_ref[...], preferred_element_type=F32)
        pre = pre + jnp.dot(oth_ref[...], up_oth_ref[...], preferred_element_type=F32)
        pre = pre + bias_ref[...]
        square = pre * pre
        tanh = jnp.tanh(0.7978845608 * (pre + 0.044715 * pre * square))
        near = 0.5 * (1.0 + tanh)
        active = (pre * near).astype(BF)
        slope = near + 0.5 * pre * (1.0 - tanh * tanh) * (
            0.7978845608 * (1.0 + 3.0 * 0.044715 * square)
        )
        grad = lax.dot_general(cot_ref[...], down, NT, preferred_element_type=F32) * slope
        grad = grad.astype(BF)
        y_ref[...] = y_ref[...] + jnp.dot(active, down, preferred_element_type=F32)
        gd_ref[0] = outer_sum(active, cot_ref[...]).astype(BF)
        gu_own_ref[...] = jnp.dot(own_t[...], grad, preferred_element_type=F32).astype(BF)
        gu_oth_ref[...] = jnp.dot(oth_t[...], grad, preferred_element_type=F32).astype(BF)
        gb_ref[...] = jnp.sum(grad.astype(F32), 0, keepdims=True)
        gs_own_ref[...] = gs_own_ref[...] + times_rows(grad, up_own_ref[...])
        gs_oth_ref[...] = gs_oth_ref[...] + times_rows(grad, up_oth_ref[...])

    @pl.when(step < half)
    def _():
        one(down_own_ref, gd_own_ref)

    @pl.when(step >= half)
    def _():
        one(down_oth_ref, gd_oth_ref)


def feed(me, owns, oths, cot, up_own, up_oth, down_own, down_oth, bias):
    sequences = len(owns)
    length, half_width = owns[0].shape
    tokens, model_width = cot.shape
    ff_width = up_own.shape[1]
    z_size, block, _ = down_own.shape

    def column(j, me_ref):
        mine = me_ref[0]
        return (0, (j % z_size) * 2 + jnp.where(j < z_size, mine, 1 - mine))

    whole = lambda j, me_ref: (0, 0)
    first = lambda j, me_ref: (jnp.minimum(j, z_size - 1), 0, 0)
    second = lambda j, me_ref: (jnp.maximum(j - z_size, 0), 0, 0)
    halves = [pl.BlockSpec((tokens, half_width), whole)] * 2
    pieces = [pl.BlockSpec((length, half_width), whole)] * (2 * sequences)
    columns = [pl.BlockSpec((half_width, block), column)] * 2
    downs = [pl.BlockSpec((1, block, model_width), first), pl.BlockSpec((1, block, model_width), second)]
    line = pl.BlockSpec((1, block), column)
    all_rows = pl.BlockSpec((tokens, model_width), whole)
    return pl.pallas_call(
        functools.partial(feed_kernel, sequences),
        grid_spec=pltpu.PrefetchScalarGridSpec(
            num_scalar_prefetch=1,
            grid=(2 * z_size,),
            in_specs=[*pieces, all_rows, *columns, *downs, line],
            out_specs=[all_rows, *halves, *downs, *columns, line],
            scratch_shapes=[pltpu.VMEM((tokens, half_width), BF)] * 2
            + [pltpu.VMEM((half_width, tokens), BF)] * 2,
        ),
        out_shape=[
            jax.ShapeDtypeStruct((tokens, model_width), F32),
            jax.ShapeDtypeStruct((tokens, half_width), F32),
            jax.ShapeDtypeStruct((tokens, half_width), F32),
            jax.ShapeDtypeStruct(down_own.shape, BF),
            jax.ShapeDtypeStruct(down_own.shape, BF),
            jax.ShapeDtypeStruct(up_own.shape, BF),
            jax.ShapeDtypeStruct(up_own.shape, BF),
            jax.ShapeDtypeStruct((1, ff_width), F32),
        ],
        compiler_params=pltpu.CompilerParams(vmem_limit_bytes=VMEM_BYTES),
        cost_estimate=LIGHT,
        name="feed",
    )(me, *owns, *oths, cot, up_own, up_oth, down_own, down_oth, bias)


def project_kernel(x_ref, gain_ref, shift_ref, w_ref, bias_ref, low_ref, q_ref, k_ref, v_ref, kt_ref, vt_ref):
    width = q_ref.shape[1]
    low = layer_norm(x_ref[...].astype(F32), gain_ref[...], shift_ref[...]).astype(BF)
    low_ref[...] = low
    made = (jnp.dot(low, w_ref[...], preferred_element_type=F32) + bias_ref[...]).astype(BF)
    made = made.astype(F32)
    keys, values = made[:, width : 2 * width], made[:, 2 * width :]
    q_ref[...] = (made[:, :width] * (HD**-0.5)).astype(BF)
    k_ref[...] = keys.astype(BF)
    v_ref[...] = values.astype(BF)
    kt_ref[...] = keys.T.astype(BF)
    vt_ref[...] = values.T.astype(BF)


def project(rows, gain, shift, weight, bias):
    length, model_width = rows.shape
    width = weight.shape[1] // 3
    block = min(512, length)
    whole = lambda i: (0, 0)
    down = lambda i: (i, 0)
    across = lambda i: (0, i)
    return pl.pallas_call(
        project_kernel,
        grid=(length // block,),
        in_specs=[
            pl.BlockSpec((block, model_width), down),
            pl.BlockSpec((1, model_width), whole),
            pl.BlockSpec((1, model_width), whole),
            pl.BlockSpec((model_width, 3 * width), whole),
            pl.BlockSpec((1, 3 * width), whole),
        ],
        out_specs=[
            pl.BlockSpec((block, model_width), down),
            pl.BlockSpec((block, width), down),
            pl.BlockSpec((block, width), down),
            pl.BlockSpec((block, width), down),
            pl.BlockSpec((width, block), across),
            pl.BlockSpec((width, block), across),
        ],
        out_shape=[jax.ShapeDtypeStruct((length, model_width), BF)]
        + [jax.ShapeDtypeStruct((length, width), BF)] * 3
        + [jax.ShapeDtypeStruct((width, length), BF)] * 2,
        compiler_params=pltpu.CompilerParams(vmem_limit_bytes=VMEM_BYTES),
        cost_estimate=LIGHT,
        name="project",
    )(rows, gain, shift, weight, bias)


def tile_helpers(head, slope, block, width):
    lane = lax.broadcasted_iota(jnp.int32, (block, width), 1)
    mine = (lane >= head * HD) & (lane < head * HD + HD)
    key = lax.broadcasted_iota(jnp.int32, (block, block), 0)
    query = lax.broadcasted_iota(jnp.int32, (block, block), 1)
    return mine, slope * key.astype(F32), key <= query


def attend_kernel(slope_ref, q_ref, k_ref, vt_ref, o_ref, lse_ref, score_scr, out_scr):
    block, width = q_ref.shape
    number, head = pl.program_id(0), pl.program_id(1)
    slope = slope_ref[head]
    mine, bias, causal = tile_helpers(head, slope, block, width)
    queries = jnp.where(mine, q_ref[...], jnp.zeros_like(q_ref[...]))

    def one_block(last):
        highest = None
        for t in range(last + 1):
            rows = pl.ds(t * block, block)
            scores = lax.dot_general(k_ref[rows, :], queries, NT, preferred_element_type=F32) + bias
            if t == last:
                scores = jnp.where(causal, scores, -1e30)
            score_scr[rows, :] = scores
            top = jnp.max(scores, 0, keepdims=True) + slope * (t * block)
            highest = top if highest is None else jnp.maximum(highest, top)
        total = jnp.zeros((1, block), F32)
        blended = jnp.zeros((width, block), F32)
        for t in range(last + 1):
            rows = pl.ds(t * block, block)
            weights = jnp.exp(score_scr[rows, :] - (highest - slope * (t * block)))
            total = total + jnp.sum(weights, 0, keepdims=True)
            blended = blended + jnp.dot(
                vt_ref[:, rows], weights.astype(BF), preferred_element_type=F32
            )
        lse_ref[...] = (highest + jnp.log(total)).reshape(lse_ref.shape)
        result = jnp.where(mine, (blended / total).T, 0.0)

        @pl.when(head == 0)
        def _():
            out_scr[...] = result

        @pl.when(head > 0)
        def _():
            out_scr[...] = out_scr[...] + result

    for last in range(k_ref.shape[0] // block):
        pl.when(number == last)(functools.partial(one_block, last))

    @pl.when(head == pl.num_programs(1) - 1)
    def _():
        o_ref[...] = out_scr[...].astype(BF)


def attend(slopes, queries, keys, values_t):
    length, width = queries.shape
    heads = slopes.shape[0]
    block = min(256, length)
    whole = lambda i, h: (0, 0)
    down = lambda i, h: (i, 0)
    return pl.pallas_call(
        attend_kernel,
        grid=(length // block, heads),
        in_specs=[
            pl.BlockSpec(memory_space=pltpu.SMEM),
            pl.BlockSpec((block, width), down),
            pl.BlockSpec((length, width), whole),
            pl.BlockSpec((width, length), whole),
        ],
        out_specs=[
            pl.BlockSpec((block, width), down),
            pl.BlockSpec((1, 1, block), lambda i, h: (h, 0, i)),
        ],
        out_shape=[
            jax.ShapeDtypeStruct((length, width), BF),
            jax.ShapeDtypeStruct((heads, 1, length), F32),
        ],
        scratch_shapes=[pltpu.VMEM((length, block), F32), pltpu.VMEM((block, width), F32)],
        compiler_params=pltpu.CompilerParams(vmem_limit_bytes=VMEM_BYTES),
        cost_estimate=LIGHT,
        name="attend",
    )(slopes, queries, keys, values_t)


def attend_back_kernel(
    slope_ref, q_ref, k_ref, kt_ref, v_ref, g_ref, lse_ref, wq_ref, wk_ref, wv_ref,
    dq_ref, dk_ref, dv_ref, first_ref, prob_scr, dp_scr, dk_scr, dv_scr, dq_scr,
):
    block, width = q_ref.shape
    number, head = pl.program_id(0), pl.program_id(1)
    slope = slope_ref[head]
    mine, bias, causal = tile_helpers(head, slope, block, width)
    queries = jnp.where(mine, q_ref[...], jnp.zeros_like(q_ref[...]))
    grads = jnp.where(mine, g_ref[...], jnp.zeros_like(g_ref[...]))
    lse = lse_ref[...].reshape(1, block)

    @pl.when((number == 0) & (head == 0))
    def _():
        dk_scr[...] = jnp.zeros_like(dk_scr)
        dv_scr[...] = jnp.zeros_like(dv_scr)

    def one_block(last):
        centre = jnp.zeros((1, block), F32)
        for t in range(last + 1):
            rows = pl.ds(t * block, block)
            scores = lax.dot_general(k_ref[rows, :], queries, NT, preferred_element_type=F32) + bias
            if t == last:
                scores = jnp.where(causal, scores, -1e30)
            probs = jnp.exp(scores - (lse - slope * (t * block)))
            dp = lax.dot_general(v_ref[rows, :], grads, NT, preferred_element_type=F32)
            prob_scr[rows, :] = probs
            dp_scr[rows, :] = dp
            centre = centre + jnp.sum(probs * dp, 0, keepdims=True)
            dv_scr[rows, :] = dv_scr[rows, :] + jnp.dot(
                probs.astype(BF), grads, preferred_element_type=F32
            )
        dq = jnp.zeros((width, block), F32)
        for t in range(last + 1):
            rows = pl.ds(t * block, block)
            ds = (prob_scr[rows, :] * (dp_scr[rows, :] - centre)).astype(BF)
            dk_scr[rows, :] = dk_scr[rows, :] + jnp.dot(ds, queries, preferred_element_type=F32)
            dq = dq + jnp.dot(kt_ref[:, rows], ds, preferred_element_type=F32)
        result = jnp.where(mine, (dq * (HD**-0.5)).T, 0.0)

        @pl.when(head == 0)
        def _():
            dq_scr[...] = result

        @pl.when(head > 0)
        def _():
            dq_scr[...] = dq_scr[...] + result

    for last in range(k_ref.shape[0] // block):
        pl.when(number == last)(functools.partial(one_block, last))

    @pl.when(head == pl.num_programs(1) - 1)
    def _():
        dq_ref[pl.ds(pl.multiple_of(number * block, block), block), :] = dq_scr[...].astype(BF)

    @pl.when((head == pl.num_programs(1) - 1) & (number == pl.num_programs(0) - 1))
    def _():
        dk_ref[...] = dk_scr[...].astype(BF)
        dv_ref[...] = dv_scr[...].astype(BF)

        def one_part(t, carry):
            rows = pl.ds(pl.multiple_of(t * block, block), block)
            first = times_rows(dq_ref[rows, :], wq_ref[...])
            first = first + times_rows(dk_ref[rows, :], wk_ref[...])
            first = first + times_rows(dv_ref[rows, :], wv_ref[...])
            first_ref[rows, :] = first.astype(BF)
            return carry

        lax.fori_loop(0, k_ref.shape[0] // block, one_part, 0)


def attend_back(slopes, queries, keys, keys_t, values, grads, lse, weights):
    length, width = queries.shape
    model_width = weights[0].shape[0]
    heads = slopes.shape[0]
    block = min(256, length)
    whole = lambda i, h: (0, 0)
    down = lambda i, h: (i, 0)
    return pl.pallas_call(
        attend_back_kernel,
        grid=(length // block, heads),
        in_specs=[
            pl.BlockSpec(memory_space=pltpu.SMEM),
            pl.BlockSpec((block, width), down),
            pl.BlockSpec((length, width), whole),
            pl.BlockSpec((width, length), whole),
            pl.BlockSpec((length, width), whole),
            pl.BlockSpec((block, width), down),
            pl.BlockSpec((1, 1, block), lambda i, h: (h, 0, i)),
        ]
        + [pl.BlockSpec((model_width, width), whole)] * 3,
        out_specs=[pl.BlockSpec((length, width), whole)] * 3
        + [pl.BlockSpec((length, model_width), whole)],
        out_shape=[jax.ShapeDtypeStruct((length, width), BF)] * 3
        + [jax.ShapeDtypeStruct((length, model_width), BF)],
        scratch_shapes=[
            pltpu.VMEM((length, block), F32),
            pltpu.VMEM((length, block), F32),
            pltpu.VMEM((length, width), F32),
            pltpu.VMEM((length, width), F32),
            pltpu.VMEM((block, width), F32),
        ],
        compiler_params=pltpu.CompilerParams(vmem_limit_bytes=VMEM_BYTES),
        cost_estimate=HEAVY,
        name="attend_back",
    )(slopes, queries, keys, keys_t, values, grads, lse, *weights)


def body(
    hidden_in,
    norm1_gain,
    norm1_bias,
    qkv_weight,
    qv_bias,
    alibi_slopes,
    out_weight,
    out_bias,
    norm2_gain,
    norm2_bias,
    up_weight,
    up_bias,
    down_weight,
    down_bias,
    out_grad,
):
    seq_devices = lax.axis_size(SEQ)
    fsdp_devices = lax.axis_size(FSDP)
    devices = seq_devices * fsdp_devices
    z_size, y_size, x_size = lax.axis_size("z"), lax.axis_size("fy"), lax.axis_size("fx")
    sequences, local_len, model_width = hidden_in.shape
    tokens = sequences * local_len
    heads_local = H // seq_devices
    width = heads_local * HD
    ff_width = up_weight.shape[1]
    rows_each = qkv_weight.shape[0]
    ff_each = down_weight.shape[0]
    place = lax.axis_index(SEQ)
    slopes = lax.dynamic_slice_in_dim(alibi_slopes, place * heads_local, heads_local)

    me = lax.axis_index("core")

    small_parts = (norm1_gain, norm1_bias, qv_bias, out_bias, norm2_gain, norm2_bias, up_bias, down_bias)
    small_here = jnp.concatenate(small_parts)
    small_all = lax.all_to_all(
        jnp.broadcast_to(small_here, (devices, small_here.shape[0])), ALL, split_axis=0, concat_axis=0, tiled=True
    )
    full, start = [], 0
    for part in small_parts:
        size = part.shape[0]
        full.append(small_all[:, start : start + size].reshape(-1).astype(F32))
        start += size
    first_gain, first_shift, bias_qv, b_out, second_gain, second_shift, b_up, b_down = full

    columns = qkv_weight.reshape(rows_each, 3, seq_devices, width).transpose(2, 0, 1, 3)
    columns = columns.reshape(seq_devices, rows_each, 3 * width)
    columns = lax.all_to_all(columns, SEQ, split_axis=0, concat_axis=0, tiled=True)
    w_heads = lax.all_gather(columns, FSDP, axis=1, tiled=False).reshape(model_width, 3 * width)
    bias_parts = bias_qv.reshape(2, seq_devices, width)
    bias_mine = lax.dynamic_index_in_dim(bias_parts, place, 1, keepdims=False)
    bias_heads = jnp.concatenate([bias_mine[0], jnp.zeros((width,), F32), bias_mine[1]])

    low_z = lax.all_gather(jnp.concatenate([out_weight, down_weight], 0), "z", axis=0, tiled=False)
    down_z, out_z = low_z[:, rows_each:], low_z[:, :rows_each]
    middle_z = z_size // 2

    def first_stage(pieces):
        return [send_axis(part, first, 1) for part, first, _ in pieces]

    def second_stage(pieces, sent):
        pairs = [join_axis(part, other, first, 1) for (part, first, _), other in zip(pieces, sent)]
        return pairs, [send_axis(p, second, at_of(second)) for p, (_, _, second) in zip(pairs, pieces)]

    def at_of(second):
        return 1 if second == "fy" else 2

    def finish(pieces, pairs, sent):
        return [join_axis(p, o, second, at_of(second)) for p, o, (_, _, second) in zip(pairs, sent, pieces)]

    low_pieces = [
        (down_z[:middle_z], "fy", "fx"), (down_z[middle_z:], "fx", "fy"), (out_z, "fy", "fx")
    ]
    low_sent = lax.optimization_barrier(first_stage(low_pieces))
    up_z = line_gather(up_weight, "z", (small_all, columns), (w_heads, *low_sent))
    low_pairs, low_sent = second_stage(low_pieces, low_sent)
    up_z = after(up_z, *low_pairs)
    up_pieces = [(up_z[:middle_z], "fy", "fx"), (up_z[middle_z:], "fx", "fy")]
    up_sent = first_stage(up_pieces)

    kept = []
    returned = []
    ahead = (up_z, *low_pairs)
    for n in range(sequences):
        rows = after(lax.all_gather(hidden_in[n], SEQ, axis=0, tiled=True), *ahead)
        first_low, q, k, v, kt, vt = project(
            rows, first_gain[None], first_shift[None], w_heads, bias_heads[None]
        )
        q_here = after(q, returned[-1]) if returned else q
        attended, lse = attend(slopes, q_here, k, vt)
        attended = attended.reshape(seq_devices, local_len, width)
        returned.append(lax.all_to_all(attended, SEQ, split_axis=0, concat_axis=0, tiled=True))
        kept.append((first_low, q, k, v, kt, lse))
        ahead = ()
        if n == 0:
            up_sent, low_sent, _ = lax.optimization_barrier((up_sent, low_sent, lse))
            up_pairs, up_sent = second_stage(up_pieces, up_sent)
            down_a, down_b, out_own = finish(low_pieces, low_pairs, low_sent)
            down_own = jnp.concatenate([down_a, down_b], 0)
            down_oth, out_oth = swap(down_own, "core"), swap(out_own, "core")
            ahead = (*ahead, *up_pairs, down_own, out_own)
    up_sent, down_oth, out_oth, _ = lax.optimization_barrier((up_sent, down_oth, out_oth, lse))
    up_own = jnp.concatenate(finish(up_pieces, up_pairs, up_sent), 0)
    up_oth = swap(up_own, "core")
    half_width = model_width // 2
    up_own, up_oth = (w.reshape(half_width, ff_width) for w in (up_own, up_oth))
    down_own, down_oth = (w.reshape(z_size, -1, model_width) for w in (down_own, down_oth))
    out_own, out_oth = (w.reshape(z_size, -1, model_width) for w in (out_own, out_oth))

    mine_core = me.reshape(1)
    middles, owns, oths = zip(
        *[
            branch(
                mine_core, returned[n], hidden_in[n], out_own, out_oth,
                b_out[None], second_gain[None], second_shift[None],
            )
            for n in range(sequences)
        ]
    )
    cot_low = out_grad.reshape(tokens, model_width)
    y, gs_own, gs_oth, gd_own, gd_oth, gu_own, gu_oth, grad_up_bias = feed(
        mine_core, owns, oths, cot_low, up_own, up_oth, down_own, down_oth, b_up[None]
    )

    cells = (z_size, y_size, x_size)
    to_up = gu_own.reshape(*cells, rows_each, ff_width)
    to_down = gd_own.reshape(*cells, ff_each, model_width)
    sum_up = [to_up, swap(gu_oth, "core").reshape(to_up.shape)]
    sum_down = [to_down, swap(gd_oth, "core").reshape(to_down.shape)]

    block_out = None
    grad_middles, grad_branches, grad_heads, sums = [], [], [], []
    for n in range(sequences):
        grad_middle, grad_branch, grad_att, four, block_out = middle_back(
            n, sequences, mine_core, gs_own, gs_oth, middles[n], out_grad[n], y,
            b_down[None], second_gain[None], out_own, out_oth, block_out,
        )
        grad_middles.append(grad_middle)
        grad_branches.append(grad_branch)
        sums.append(four)
        grad_heads.append(lax.all_to_all(grad_att, SEQ, split_axis=0, concat_axis=0, tiled=True))
    go_own, go_oth = out_weight_grad(mine_core, returned, grad_branches)
    to_out = go_own.reshape(*cells, rows_each, model_width)
    sum_out = [to_out, swap(go_oth, "core").reshape(to_out.shape)]
    parts = (give_part(sum_up, "fy", 1), give_part(sum_down, "fx", 2), give_part(sum_out, "fx", 2))
    sum_up = take_part(sum_up, parts[0], "fy", 1)
    sum_down = take_part(sum_down, parts[1], "fx", 2)
    sum_out = take_part(sum_out, parts[2], "fx", 2)

    four = total_of(sums)
    rear = [four[0], four[1], four[2], grad_up_bias, four[3]]
    grad_heads[0] = after(grad_heads[0], *parts)
    head_weights = [w_heads[:, i * width : (i + 1) * width] for i in range(3)]
    grad_first, grad_projected = [], []
    for n in range(sequences):
        first_low, q, k, v, kt, lse = kept[n]
        if n > 0:
            q = after(q, partial, *gives)
        *parts_qkv, partial = attend_back(
            slopes, q, k, kt, v, grad_heads[n].reshape(q.shape), lse, head_weights
        )
        grad_first.append(lax.psum_scatter(partial, SEQ, scatter_dimension=0, tiled=True))
        recent = [terms[-1] for terms in (sum_up, sum_down, sum_out)]
        if n < sequences - 1:
            recent.append(grad_heads[n + 1])
        parts_qkv, recent = lax.optimization_barrier((parts_qkv, recent))
        if n < sequences - 1:
            grad_heads[n + 1] = recent.pop()
        sum_up, sum_down, sum_out = (
            [*terms[:-1], term] for terms, term in zip((sum_up, sum_down, sum_out), recent)
        )
        if n == 0:
            gives = (give_part(sum_up, "fx", 1), give_part(sum_down, "fy", 1), give_part(sum_out, "fy", 1))
            sum_up = take_part(sum_up, gives[0], "fx", 1)
            sum_down = take_part(sum_down, gives[1], "fy", 1)
            sum_out = take_part(sum_out, gives[2], "fy", 1)
        grad_projected.append(jnp.concatenate(parts_qkv, 1))
    grad_qkvw = jnp.zeros((model_width, 3 * width), F32)
    column_sums = jnp.zeros((3 * width,), F32)
    for n in range(sequences):
        grad_qkvw = grad_qkvw + outer_sum(kept[n][0], grad_projected[n])
        column_sums = column_sums + jnp.sum(grad_projected[n].astype(F32), 0)
    wide = [grad_qkvw.reshape(seq_devices, y_size, x_size, rows_each, 3 * width)]
    wide = total_of(reduce_axis(reduce_axis(wide, "fy", 1), "fx", 1))
    wide = lax.all_to_all(wide, SEQ, split_axis=0, concat_axis=0, tiled=True)
    wide = wide.reshape(seq_devices, rows_each, 3, width).transpose(1, 2, 0, 3)
    out_qkvw = wide.reshape(rows_each, 3 * model_width)

    low_sum = jnp.concatenate([total_of(sum_out).astype(BF), total_of(sum_down).astype(BF)], 1)
    low_sum = line_reduce(low_sum, "z")
    out_outw, out_down = low_sum[:rows_each], low_sum[rows_each:]
    out_up = line_reduce(total_of(sum_up).astype(BF), "z")

    input_grad = None
    for n in range(sequences):
        input_grad = first_back(
            n, sequences, grad_first[n], hidden_in[n], first_gain[None], grad_middles[n], input_grad
        )

    rear_wide = jnp.concatenate([part.reshape(devices, -1) for part in rear], 1)
    columns_wide = jnp.broadcast_to(column_sums, (devices, 3 * width))
    small = jnp.concatenate([rear_wide, columns_wide], 1)
    small = lax.all_to_all(small, ALL, split_axis=0, concat_axis=0, tiled=True)
    rear_sum = jnp.sum(small[:, : rear_wide.shape[1]], 0)
    rear_outs, start = [], 0
    for part in rear:
        size = part.size // devices
        rear_outs.append(rear_sum[start : start + size])
        start += size
    out_bias_sum, gain_two, shift_two, up_bias_sum, down_bias_sum = rear_outs
    totals = small[:, start:].reshape(seq_devices, fsdp_devices, 3, width).sum(1).transpose(1, 0, 2)
    totals = totals.reshape(3, model_width)
    qv_each = qv_bias.shape[0]
    qv = lax.dynamic_slice_in_dim(totals[::2].reshape(-1), lax.axis_index(ALL) * qv_each, qv_each)
    weight_here = qkv_weight.astype(F32)
    shift_one = jnp.sum(weight_here * totals.reshape(-1), 1)
    gain_one = jnp.sum(weight_here * out_qkvw, 1) - norm1_bias.astype(F32) * shift_one
    gain_one = gain_one / norm1_gain.astype(F32)
    return (
        block_out, input_grad, gain_one, shift_one, out_qkvw, qv, out_outw, out_bias_sum,
        gain_two, shift_two, out_up, up_bias_sum, out_down, down_bias_sum,
    )


def solution(mesh):
    seq_size, fsdp_size = mesh.shape["seq"], mesh.shape["fsdp"]
    fine = Mesh(mesh.devices.reshape(seq_size // 2, 2, fsdp_size // 2, 2), ALL)
    tokens = P(FSDP, SEQ, None)
    vector = P(ALL)
    matrix = P(ALL, None)
    return jax.shard_map(
        body,
        mesh=fine,
        in_specs=(
            tokens, vector, vector, matrix, vector, P(), matrix, vector, vector, vector,
            matrix, vector, matrix, vector, tokens,
        ),
        out_specs=(
            tokens, tokens, vector, vector, matrix, vector, matrix, vector, vector, vector,
            matrix, vector, matrix, vector,
        ),
        check_vma=False,
    )
```
